512 devices in a mesh: dp: 32 (over y, z_lo, core), tensor: 16 (over x, z_hi).
Axes of the slice: x: 4, y: 4, z: 16 (z_hi: 4, z_lo: 4; z = z_hi * 4 + z_lo), core: 2. Of those that a mesh axis runs over, the one named last changes fastest.
Arguments:
- tokens: bfloat16 [131072, 4096], P(('dp', 'tensor')), may hold values from -6 to 6
- cotangent: bfloat16 [131072, 4096], P(('dp', 'tensor')), may hold values from -0.29882812 to 0.29882812
- routes: int32 [131072, 8], P(('dp', 'tensor')), may hold values from 0 to 127, as said below
- combine: float32 [131072, 8], P(('dp', 'tensor')), may hold values from 0.05 to 1
- gate_up_codes: int32 [2, 4096, 4096], P(None, 'tensor', 'dp'), may hold values from 0 to 15
- gate_up_scales: float32 [2, 4096, 128], P(None, 'tensor', 'dp'), may hold values from 0.003 to 0.01
- down_codes: int32 [4096, 4096], P('tensor', 'dp'), may hold values from 0 to 15
- down_scales: float32 [128, 4096], P('tensor', 'dp'), may hold values from 0.004 to 0.016
Outputs:
- gate_up_grad: float32 [2, 4096, 4096], P(None, 'tensor', 'dp')
- gate_up_scale_grad: float32 [2, 4096, 128], P(None, 'tensor', 'dp')
The draws below stay inside these ranges and needn't reach their ends.
Inputs may be any that keep to these rules, and one draw needn't show every extreme that they name: `routes`: each row names 8 different experts. For each expert e < 4, in the rows of one device at most 20 name e, and in every draw the rows of some device have exactly 20 that name e.
All inputs are finite; a program needn't handle non-finite values.
Results may differ from the reference program's by a relative error of at most 0.029.
Values may be sent and summed in bfloat16 or wider, within the bound.
A program may use at most 64 MiB of HBM per device.

```python
import math
from functools import partial
import jax
import jax.numpy as jnp
from jax import lax

D = 4096
EXPERTS = 128
TOP = 8
BLOCK = 32
WIN = 1024
TOK_DEV = 256
CAP = 20
EXP_WIN = 4
UNITS = 4096
TOKENS = 131072
N_DP = 32
N_TENSOR = 16


def draw_routes(key, part):
    key = jax.random.fold_in(key, 11)
    key_other, key_count, key_filled, key_pick, key_order, key_slot = jax.random.split(key, 6)
    blocks = TOKENS // TOK_DEV
    rest = EXPERTS - EXP_WIN
    scores = jax.random.randint(key_other, (TOKENS, rest), 0, 2 ** 20) * EXPERTS + jnp.arange(rest, dtype=jnp.int32)[None, :]
    others = lax.top_k(scores, TOP)[1].astype(jnp.int32) + EXP_WIN
    divisor = jax.random.randint(key_count, (blocks, EXP_WIN), 1, 9)
    counts = CAP // divisor
    picked_block = jax.random.randint(key_pick, (EXP_WIN,), 0, blocks)
    filled = (jax.random.randint(key_filled, (blocks, EXP_WIN), 0, 4) == 0) | (jnp.arange(blocks, dtype=jnp.int32)[:, None] == picked_block[None, :])
    counts = jnp.where(filled, CAP, counts)
    block_keys = jax.random.split(key_order, blocks * EXP_WIN)
    ranking = jax.vmap(lambda one_key: jax.random.permutation(one_key, TOK_DEV))(block_keys).reshape(blocks, EXP_WIN, TOK_DEV)
    selected = jnp.transpose(ranking < counts[:, :, None], (0, 2, 1)).reshape(TOKENS, EXP_WIN)
    slot_scores = jax.random.randint(key_slot, (TOKENS, TOP), 0, 2 ** 20) * TOP + jnp.arange(TOP, dtype=jnp.int32)[None, :]
    slot_order = jnp.argsort(slot_scores, axis=1)[:, :EXP_WIN].astype(jnp.int32)
    hits = (slot_order[:, :, None] == jnp.arange(TOP, dtype=jnp.int32)[None, None, :]) & selected[:, :, None]
    placed = jnp.any(hits, axis=1)
    expert_here = jnp.sum(jnp.where(hits, jnp.arange(EXP_WIN, dtype=jnp.int32)[None, :, None], 0), axis=1)
    return jnp.where(placed, expert_here, others).astype(jnp.int32)


def place_ends(values, rng, smallest, high):
    dims = values.shape
    spot = [jax.random.randint(jax.random.fold_in(rng, axis), (), 0, dims[axis]) for axis in range(len(dims))]
    values = values.at[tuple(spot)].set(smallest)
    longest = dims.index(max(dims))
    spot[longest] = (spot[longest] + 1) % dims[longest]
    return values.at[tuple(spot)].set(high)


def block_levels(rng, shape, cuts, least, largest):
    loudness, own = 1.0, jax.random.fold_in(rng, 6)
    for axis_at, blocks in cuts:
        heights = jnp.exp(jax.random.uniform(jax.random.fold_in(own, axis_at), (blocks,), jnp.float32, least / len(cuts), largest / len(cuts)))
        loudness = loudness * jnp.repeat(heights, shape[axis_at] // blocks).reshape([-1 if axis == axis_at else 1 for axis in range(len(shape))])
    return loudness


def noise(rng, shape, deviation, bound, cuts=(), held_as=jnp.bfloat16):
    result = jax.random.normal(rng, shape, jnp.float32) * deviation
    if len(cuts) > 0:
        result = block_levels(rng, shape, cuts, -0.22, 0.18) * result
    return jnp.clip(result, min=-bound, max=bound).astype(held_as)


def setup_inputs(seed: int = 0) -> dict:
    keys = jax.random.split(jax.random.key(seed), 9)
    return {
        "tokens": noise(keys[0], (TOKENS, D), 1.0, 6.0, ((0, 512),)),
        "cotangent": noise(keys[1], (TOKENS, D), 0.05, 0.29882812, ((0, 512),)),
        "routes": draw_routes(jax.random.fold_in(keys[8], 71), 0),
        "combine": jnp.clip(jnp.exp(math.log(1.0) - 2.9957323 * jax.random.uniform(keys[3], (TOKENS, TOP), jnp.float32) ** block_levels(keys[3], (TOKENS, TOP), ((0, 512),), -0.2, 0.2)), 0.05, 1.0),
        "gate_up_codes": place_ends(jax.random.randint(keys[4], (2, UNITS, D), 0, 16), jax.random.fold_in(keys[4], 1), 0, 15).astype(jnp.int32),
        "gate_up_scales": jnp.clip(jnp.exp(math.log(0.01) - 1.2039728 * jax.random.uniform(keys[5], (2, UNITS, D // BLOCK), jnp.float32) ** block_levels(keys[5], (2, UNITS, D // BLOCK), ((1, 16), (2, 32)), -0.2, 0.2)), 0.003, 0.01),
        "down_codes": place_ends(jax.random.randint(keys[6], (UNITS, D), 0, 16), jax.random.fold_in(keys[6], 1), 0, 15).astype(jnp.int32),
        "down_scales": jnp.clip(jnp.exp(math.log(0.016) - 1.3862944 * jax.random.uniform(keys[7], (UNITS // BLOCK, D), jnp.float32) ** block_levels(keys[7], (UNITS // BLOCK, D), ((0, 16), (1, 32)), -0.2, 0.2)), 0.004, 0.016),
    }


lsq_factor = 192.0 ** -0.5


def decode_values(code_array):
    modulus = (code_array % 8).astype(jnp.float32)
    levels = jnp.where(modulus < 4.0, 0.5 * modulus, jnp.where(modulus < 6.0, modulus - 2.0, jnp.where(modulus < 7.0, 4.0, 6.0)))
    sign_part = 1.0 - 2.0 * (code_array // 8).astype(jnp.float32)
    return sign_part * levels


def select_rows(routes, combine, expert_count, capacity):
    chosen = routes[:, :, None] == jnp.arange(expert_count, dtype=jnp.int32)[None, None, :]
    is_routed = jnp.any(chosen, axis=1)
    weight = jnp.sum(jnp.where(chosen, combine[:, :, None], jnp.zeros_like(combine)[:, :, None]), axis=1)
    slot_index = jnp.cumsum(is_routed.astype(jnp.int32), axis=0) - 1
    one_hot = (slot_index.T[:, None, :] == jnp.arange(capacity, dtype=jnp.int32)[None, :, None]) & is_routed.T[:, None, :]
    return one_hot.astype(jnp.float32), weight


def reference(tokens, cotangent, routes, combine, gate_up_codes, gate_up_scales, down_codes, down_scales):
    gate_up_values = decode_values(gate_up_codes)
    down_values = decode_values(down_codes)
    gate_up_weight = (gate_up_values.reshape(2, UNITS, D // BLOCK, BLOCK) * gate_up_scales[..., None]).reshape(2, UNITS, D).astype(jnp.bfloat16)
    down_weight = (down_values.reshape(UNITS // BLOCK, BLOCK, D) * down_scales[:, None, :]).reshape(UNITS, D).astype(jnp.bfloat16)
    gate_up_wide = gate_up_weight.astype(jnp.float32).reshape(2, EXP_WIN, WIN, D)
    down_wide = down_weight.astype(jnp.float32).reshape(EXP_WIN, WIN, D)
    group_rows = N_TENSOR * TOK_DEV
    selector = partial(select_rows, expert_count=EXP_WIN, capacity=CAP)

    def one_group(running, group_index):
        first_row = (group_index * group_rows).astype(jnp.int32)
        group_tokens = lax.dynamic_slice_in_dim(tokens, first_row, group_rows, 0).reshape(N_TENSOR, TOK_DEV, D).astype(jnp.float32)
        group_cot = lax.dynamic_slice_in_dim(cotangent, first_row, group_rows, 0).reshape(N_TENSOR, TOK_DEV, D).astype(jnp.float32)
        group_routes = lax.dynamic_slice_in_dim(routes, first_row, group_rows, 0).reshape(N_TENSOR, TOK_DEV, TOP)
        group_combine = lax.dynamic_slice_in_dim(combine, first_row, group_rows, 0).reshape(N_TENSOR, TOK_DEV, TOP)
        one_hot, weight = jax.vmap(selector)(group_routes, group_combine)
        token_rows = jnp.einsum("necT,nTd->encd", one_hot, group_tokens).reshape(EXP_WIN, N_TENSOR * CAP, D)
        cot_rows = jnp.einsum("necT,nTd->encd", one_hot, group_cot).reshape(EXP_WIN, N_TENSOR * CAP, D)
        picked_weight = jnp.einsum("necT,nTe->enc", one_hot, weight).reshape(EXP_WIN, N_TENSOR * CAP)
        scaled_low = (picked_weight[:, :, None] * cot_rows).astype(jnp.bfloat16)
        scaled_rows = lax.optimization_barrier(scaled_low).astype(jnp.float32)
        projected = jnp.einsum("erd,gefd->gerf", token_rows, gate_up_wide)
        back_hidden = jnp.einsum("erd,efd->erf", scaled_rows, down_wide)
        pre_gate = projected[0]
        pre_up = projected[1]
        sigmoid_gate = jax.nn.sigmoid(pre_gate)
        silu_gate = pre_gate * sigmoid_gate
        grad_gate = (back_hidden * pre_up * sigmoid_gate * (1.0 + pre_gate * (1.0 - sigmoid_gate))).astype(jnp.bfloat16)
        grad_up = (back_hidden * silu_gate).astype(jnp.bfloat16)
        rounded_grads = lax.optimization_barrier((grad_gate, grad_up))
        grad_pair = jnp.stack([rounded_grads[0], rounded_grads[1]]).astype(jnp.float32)
        partial_sum = jnp.einsum("gerf,erd->gefd", grad_pair, token_rows).reshape(2, UNITS, D)
        rounded = lax.optimization_barrier(partial_sum.astype(jnp.bfloat16)).astype(jnp.float32)
        return running + rounded, None

    summed, ignored = lax.scan(one_group, jnp.zeros((2, UNITS, D), jnp.float32), jnp.arange(N_DP, dtype=jnp.int32))
    gate_up_grad = jnp.where(gate_up_codes % 8 != 7, summed, jnp.zeros_like(summed))
    gate_up_scale_grad = lsq_factor * jnp.sum((summed * gate_up_values).reshape(2, UNITS, D // BLOCK, BLOCK), axis=-1)
    return gate_up_grad, gate_up_scale_grad
```

```python
import jax
import jax.numpy as jnp
from jax import lax
from jax.sharding import Mesh
from jax.sharding import PartitionSpec as P

BLOCK = 32
CAP = 20
SIDE = 4
SWAP = [(p * SIDE + q, q * SIDE + p) for p in range(SIDE) for q in range(SIDE)]


lsq_factor = 192.0 ** (-0.5)


def decode_values(code_array):
    modulus = (code_array % 8).astype(jnp.float32)
    levels = jnp.where(
        modulus < 4.0,
        0.5 * modulus,
        jnp.where(modulus < 6.0, modulus - 2.0, jnp.where(modulus < 7.0, 4.0, 6.0)),
    )
    sign_part = 1.0 - 2.0 * (code_array // 8).astype(jnp.float32)
    return sign_part * levels


def body(
    tokens, cotangent, routes, combine, gate_up_codes, gate_up_scales, down_codes, down_scales
):
    expert_count = lax.axis_size("x")
    expert_ids = jnp.arange(expert_count, dtype=jnp.int32)
    chosen = routes[:, :, None] == expert_ids[None, None, :]
    is_routed = jnp.any(chosen, axis=1)
    weight = jnp.sum(
        jnp.where(chosen, combine[:, :, None], jnp.zeros_like(combine)[:, :, None]), axis=1
    )
    slot_index = jnp.cumsum(is_routed.astype(jnp.int32), axis=0) - 1
    one_hot = (
        slot_index.T[:, None, :] == jnp.arange(CAP, dtype=jnp.int32)[None, :, None]
    ) & is_routed.T[:, None, :]
    selector = one_hot.astype(jnp.bfloat16)
    picked_tokens = jnp.einsum(
        "ect,td->ecd", selector, tokens, preferred_element_type=jnp.float32
    ).astype(jnp.bfloat16)
    picked_cot = jnp.einsum("ect,td->ecd", selector, cotangent, preferred_element_type=jnp.float32)
    picked_weight = jnp.sum(one_hot.astype(jnp.float32) * weight.T[:, None, :], axis=2)
    picked_scaled = (picked_weight[:, :, None] * picked_cot).astype(jnp.bfloat16)
    picked = jnp.stack([picked_tokens, picked_scaled], axis=1)
    own_expert = lax.all_to_all(picked, "x", split_axis=0, concat_axis=0, tiled=True)
    pooled = lax.all_gather(own_expert, ("y", "c"), axis=0, tiled=True)
    token_block, scaled_block = pooled[:, 0], pooled[:, 1]
    width_full = tokens.shape[1]
    token_rows = token_block.reshape(-1, width_full)
    scaled_rows = scaled_block.reshape(-1, width_full)
    gate_up_values = decode_values(gate_up_codes)
    down_values = decode_values(down_codes)
    hidden_local = gate_up_codes.shape[1]
    width_local = gate_up_codes.shape[2]
    gate_up_weight = (
        (
            gate_up_values.reshape(2, hidden_local, width_local // BLOCK, BLOCK)
            * gate_up_scales[..., None]
        )
        .reshape(2, hidden_local, width_local)
        .astype(jnp.bfloat16)
    )
    down_weight = (
        (down_values.reshape(hidden_local // BLOCK, BLOCK, width_local) * down_scales[:, None, :])
        .reshape(hidden_local, width_local)
        .astype(jnp.bfloat16)
    )
    stacked = jnp.concatenate([gate_up_weight, down_weight[None]], axis=0)
    halves = lax.all_to_all(stacked, "c", split_axis=1, concat_axis=2, tiled=True)
    swapped = lax.ppermute(halves, ("y", "zh"), SWAP)
    gathered = lax.all_gather(swapped, ("zh", "zl"), axis=2, tiled=True)
    projected = jnp.einsum(
        "rd,gfd->grf", token_rows, gathered[:2], preferred_element_type=jnp.float32
    )
    back_hidden = jnp.einsum(
        "rd,fd->rf", scaled_rows, gathered[2], preferred_element_type=jnp.float32
    )
    pre_gate = projected[0]
    pre_up = projected[1]
    sigmoid_gate = jax.nn.sigmoid(pre_gate)
    silu_gate = pre_gate * sigmoid_gate
    grad_gate = (
        back_hidden * pre_up * sigmoid_gate * (1.0 + pre_gate * (1.0 - sigmoid_gate))
    ).astype(jnp.bfloat16)
    grad_up = (back_hidden * silu_gate).astype(jnp.bfloat16)
    grad_pair = jnp.stack([grad_gate, grad_up])
    partial_sum = jnp.einsum(
        "grf,rd->gfd", grad_pair, token_rows, preferred_element_type=jnp.float32
    )
    scattered = lax.psum_scatter(
        partial_sum.astype(jnp.bfloat16), ("zh", "zl"), scatter_dimension=2, tiled=True
    )
    back = lax.ppermute(scattered, ("y", "zh"), SWAP)
    summed = lax.all_to_all(back, "c", split_axis=2, concat_axis=1, tiled=True).astype(jnp.float32)
    gate_up_grad = jnp.where(gate_up_codes % 8 != 7, summed, jnp.zeros_like(summed))
    gate_up_scale_grad = lsq_factor * jnp.sum(
        (summed * gate_up_values).reshape(2, hidden_local, width_local // BLOCK, BLOCK), axis=-1
    )
    return (gate_up_grad, gate_up_scale_grad)


def solution(mesh):
    fine = Mesh(
        mesh.devices.reshape(SIDE, SIDE, 2, SIDE, SIDE), ("y", "zl", "c", "x", "zh")
    )
    dp, tensor = ("y", "zl", "c"), ("x", "zh")
    rows = P(dp + tensor, None)
    return jax.shard_map(
        body,
        mesh=fine,
        in_specs=(
            rows,
            rows,
            rows,
            rows,
            P(None, tensor, dp),
            P(None, tensor, dp),
            P(tensor, dp),
            P(tensor, dp),
        ),
        out_specs=(P(None, tensor, dp), P(None, tensor, dp)),
        check_vma=False,
    )
```

```python
import jax
import jax.numpy as jnp
from jax import lax
from jax.experimental import pallas as pl
from jax.experimental.pallas import tpu as pltpu
from jax.sharding import PartitionSpec as P

BLOCK = 32
CAP = 20
NX, NY, NZ, NC = 4, 4, 16, 2
SEG = 4
POOL = NY * NC
D = 4096
TOK = 256
MAIN = 16
TAIL = CAP - MAIN
QUART = D // SEG
PACK = D + QUART
HID = 256
SUB = HID // POOL
FEAT = 128
PIECE = 3 * SUB
HALF = PIECE // 2
PMAIN = POOL * MAIN
PTAIL = POOL * TAIL
ROWS = NX * PMAIN
TAILS = NX * PTAIL
WIDTH = SEG * SUB
OFFSETS = (0, 1, 3, 2)
STEPS = NZ // 2
MESH = pl.DeviceIdType.MESH
LSQ = 192.0 ** (-0.5)
F32 = jnp.float32
BF16 = jnp.bfloat16


def decode_values(code_array):
    modulus = (code_array % 8).astype(F32)
    levels = jnp.where(
        modulus < 4.0,
        0.5 * modulus,
        jnp.where(modulus < 6.0, modulus - 2.0, jnp.where(modulus < 7.0, 4.0, 6.0)),
    )
    return jnp.where(code_array >= 8, -levels, levels)


def iota(shape, axis):
    return lax.broadcasted_iota(jnp.int32, shape, axis)


def nt_dot(a, b):
    return lax.dot_general(a, b, (((1,), (1,)), ((), ())), preferred_element_type=F32)


def dot(a, b):
    return jnp.dot(a, b, preferred_element_type=F32)


def device_at(x, y, z, c):
    return (y * (SEG * NC) + lax.rem(z, SEG) * NC + c, x * SEG + z // SEG)


def kernel(
    tok_hbm,
    cot_hbm,
    routes_ref,
    combine_ref,
    gu_codes_ref,
    gu_scales_ref,
    d_codes_ref,
    d_scales_ref,
    grad_ref,
    scale_ref,
    tok_v,
    cot_v,
    sbuf,
    xbuf,
    xtail,
    wsend,
    wfull,
    pre_tail,
    g_t,
    dw,
    rs_out,
    rs_in,
    fin_out,
    fin_in,
    load_sem,
    x_s,
    x_r,
    y_s,
    y_r,
    p_s,
    p_r,
    a_s,
    a_r,
    w_s,
    w_r,
    r_s,
    r_r,
    f_s,
    f_r,
):
    dp = lax.axis_index("dp")
    tensor = lax.axis_index("tensor")
    x, zh = tensor // SEG, lax.rem(tensor, SEG)
    y, rest = dp // (SEG * NC), lax.rem(dp, SEG * NC)
    zl, c = rest // NC, lax.rem(rest, NC)
    z = zh * SEG + zl
    p = y * NC + c
    oc = 1 - c
    y_up, y_dn, y_far = lax.rem(y + 1, NY), lax.rem(y + NY - 1, NY), lax.rem(y + 2, NY)
    z_up, z_dn = lax.rem(z + 1, NZ), lax.rem(z + NZ - 1, NZ)
    to_y = (device_at(x, y_up, z, c), device_at(x, y_dn, z, c))
    to_z = (device_at(x, y, z_up, c), device_at(x, y, z_dn, c))
    partner = device_at(x, y, z, oc)

    def member(index):
        return device_at(x, index // NC, z, lax.rem(index, NC))

    def copy(src, dst, sent, got, device):
        return pltpu.make_async_remote_copy(
            src_ref=src,
            dst_ref=dst,
            send_sem=sent,
            recv_sem=got,
            device_id=device,
            device_id_type=MESH,
        )

    started = []

    def send(src, dst, sent, got, device):
        one = copy(src, dst, sent, got, device)
        one.start()
        started.append(one)

    def arrived(dst, sent, got):
        copy(dst, dst, sent, got, partner).wait_recv()

    loads = [
        pltpu.make_async_copy(tok_hbm, tok_v, load_sem.at[0]),
        pltpu.make_async_copy(cot_hbm, cot_v, load_sem.at[1]),
    ]
    for one in loads:
        one.start()

    barrier = pltpu.get_barrier_semaphore()
    peers = [member(lax.rem(p + k, POOL)) for k in range(1, POOL)]
    peers += [device_at(lax.rem(x + o, NX), y, z, c) for o in range(1, NX)]
    peers += list(to_z)
    for peer in peers:
        pl.semaphore_signal(barrier, inc=1, device_id=peer, device_id_type=MESH)

    lane_block = iota((HID, FEAT), 1) // BLOCK
    for g in range(2):
        rows = pl.ds(g * HID, HID)
        scale = jnp.zeros((HID, FEAT), F32)
        for b in range(FEAT // BLOCK):
            scale = jnp.where(lane_block == b, gu_scales_ref[rows, b : b + 1], scale)
        weight = (scale * decode_values(gu_codes_ref[rows, :])).astype(BF16)
        for m in range(POOL):
            wsend[m, g * SUB : (g + 1) * SUB, :] = weight[m * SUB : (m + 1) * SUB, :]
    for m in range(POOL):
        values = decode_values(d_codes_ref[m * SUB : (m + 1) * SUB, :])
        wsend[m, 2 * SUB : 3 * SUB, :] = (d_scales_ref[m : m + 1, :] * values).astype(BF16)

    pl.semaphore_wait(barrier, len(peers))

    def piece(origin, first=0, count=PIECE):
        row = pl.multiple_of((origin // SEG) * PIECE + first, 16)
        column = pl.multiple_of(lax.rem(origin, SEG) * QUART, QUART)
        return wfull.at[pl.ds(row, count), pl.ds(column, QUART)]

    def part(index):
        row = pl.multiple_of(zh * PIECE, 16)
        column = pl.multiple_of(zl * QUART + index * FEAT, FEAT)
        return wfull.at[pl.ds(row, PIECE), pl.ds(column, FEAT)]

    own_part = pltpu.make_async_copy(wsend.at[p], part(p), load_sem.at[2])
    own_part.start()
    for k in range(1, POOL):
        to = lax.rem(p + k, POOL)
        send(wsend.at[to], part(p), a_s.at[k - 1], a_r.at[k - 1], member(to))

    masks, weights = [], []
    for e in range(NX):
        chosen = routes_ref[...] == e
        masks.append(jnp.max(chosen.astype(F32), axis=0, keepdims=True))
        weights.append(
            jnp.sum(jnp.where(chosen, combine_ref[...], 0.0), axis=0, keepdims=True)
        )
    mask = jnp.concatenate(masks + [jnp.zeros((4, TOK), F32)], axis=0)
    before = (iota((TOK, TOK), 0) <= iota((TOK, TOK), 1)).astype(F32).astype(BF16)
    count = dot(mask.astype(BF16), before)
    place = jnp.where(mask > 0.0, count - 1.0, -1.0).astype(jnp.int32)
    wide = (MAIN, TOK)
    place = jnp.concatenate(
        [jnp.broadcast_to(place[e : e + 1], wide) for e in range(NX)], axis=0
    )
    weight = jnp.concatenate(
        [jnp.broadcast_to(weights[e], wide) for e in range(NX)], axis=0
    )
    slot = lax.rem(iota((NX * MAIN, TOK), 0), MAIN)
    is_main = place == slot
    is_tail = place == MAIN + lax.rem(slot, TAIL)
    main_weight = jnp.sum(jnp.where(is_main, weight, 0.0), axis=1, keepdims=True)
    tail_weight = jnp.sum(jnp.where(is_tail, weight, 0.0), axis=1, keepdims=True)
    pick_main = is_main.astype(F32).astype(BF16)
    pick_tail = [
        (is_tail & (slot // TAIL == k)).astype(F32).astype(BF16) for k in range(SEG)
    ]
    wide = QUART // NY
    for which, (source, load) in enumerate(zip((tok_v, cot_v), loads)):
        load.wait()
        for quarter in range(NY):
            folded = jnp.zeros((NX * MAIN, wide), F32)
            for k in range(SEG):
                first = quarter * QUART + k * wide
                values = source[:, first : first + wide]
                picked = dot(pick_main, values)
                folded = folded + dot(pick_tail[k], values)
                if which == 1:
                    picked = picked * main_weight
                to = k * QUART + quarter * wide
                sbuf[which, :, to : to + wide] = picked.astype(BF16)
            if which == 1:
                folded = folded * tail_weight
            to = D + quarter * wide
            sbuf[which, :, to : to + wide] = folded.astype(BF16)

    def for_expert(e):
        return sbuf.at[:, pl.ds(pl.multiple_of(e * MAIN, MAIN), MAIN), :]

    def rows_of(group, at_y, at_c):
        row = group * PMAIN + (at_y * NC + at_c) * MAIN
        return pl.ds(pl.multiple_of(row, MAIN), MAIN)

    def block(group, at_y, at_c):
        return xbuf.at[:, rows_of(group, at_y, at_c), :]

    def one_block(which, group, at_y, at_c):
        return xbuf.at[which, rows_of(group, at_y, at_c), :]

    own_rows = pltpu.make_async_copy(for_expert(x), block(0, y, c), load_sem.at[3])
    own_rows.start()
    for group in range(1, NX):
        e = lax.rem(x + OFFSETS[group], NX)
        send(
            for_expert(e),
            block(group, y, c),
            x_s.at[group - 1],
            x_r.at[group - 1],
            device_at(e, y, z, c),
        )

    def spread(group):
        if group == 0:
            source = for_expert(x)
        else:
            source = block(group, y, c)
            arrived(source, x_s.at[group - 1], x_r.at[group - 1])
        for way in range(2):
            send(
                source,
                block(group, y, c),
                y_s.at[0, way, group],
                y_r.at[0, way, group],
                to_y[way],
            )
        send(source, block(group, y, c), p_s.at[group, 0], p_r.at[group, 0], partner)

    def relay(group):
        for way in range(2):
            from_y = (y_dn, y_up)[way]
            whole = block(group, from_y, c)
            arrived(whole, y_s.at[0, way, group], y_r.at[0, way, group])
            half = one_block(way, group, from_y, c)
            send(half, half, y_s.at[1, way, group], y_r.at[1, way, group], to_y[way])
            send(whole, whole, p_s.at[group, 1 + way], p_r.at[group, 1 + way], partner)

    def relay_far(group):
        for way in range(2):
            half = one_block(way, group, y_far, c)
            arrived(half, y_s.at[1, way, group], y_r.at[1, way, group])
            send(half, half, p_s.at[group, 3 + way], p_r.at[group, 3 + way], partner)

    def all_rows(group):
        arrived(block(group, y, oc), p_s.at[group, 0], p_r.at[group, 0])
        arrived(block(group, y_dn, oc), p_s.at[group, 1], p_r.at[group, 1])
        arrived(block(group, y_up, oc), p_s.at[group, 2], p_r.at[group, 2])
        for way in range(2):
            half = one_block(way, group, y_far, oc)
            arrived(half, p_s.at[group, 3 + way], p_r.at[group, 3 + way])

    def weight_piece(step, way, origin):
        if step < STEPS:
            return piece(origin)
        return piece(origin, way * HALF, HALF)

    def weights_on(step):
        for way in range(2):
            back = NZ - (step - 1) if way == 0 else step - 1
            ref = weight_piece(step, way, lax.rem(z + back, NZ))
            send(ref, ref, w_s.at[way, step - 1], w_r.at[way, step - 1], to_z[way])

    def weights_in(step):
        for way in range(2):
            back = NZ - step if way == 0 else step
            ref = weight_piece(step, way, lax.rem(z + back, NZ))
            arrived(ref, w_s.at[way, step - 1], w_r.at[way, step - 1])
        if step < STEPS:
            weights_on(step + 1)

    spread(0)
    own_part.wait()
    for k in range(1, POOL):
        got = part(lax.rem(p + POOL - k, POOL))
        arrived(got, a_s.at[k - 1], a_r.at[k - 1])
    weights_on(1)

    weights_in(1)
    relay(0)
    weights_in(2)
    spread(1)
    spread(2)
    relay_far(0)
    weights_in(3)
    spread(3)
    relay(1)
    weights_in(4)
    relay_far(1)
    own_rows.wait()

    fold_from = iota((PMAIN, PMAIN), 1)
    fold_to = iota((PMAIN, PMAIN), 0)
    inside = lax.rem(fold_to, PTAIL)
    wanted = (inside // TAIL) * MAIN + (fold_to // PTAIL) * TAIL + lax.rem(inside, TAIL)
    unfold = (fold_from == wanted).astype(F32).astype(BF16)

    def unpack(group):
        all_rows(group)
        for which in range(2):
            folded = xbuf[which, group * PMAIN : (group + 1) * PMAIN, D:PACK]
            tails = dot(unfold, folded).astype(BF16)
            for k in range(SEG):
                xtail[
                    which,
                    group * PTAIL : (group + 1) * PTAIL,
                    k * QUART : (k + 1) * QUART,
                ] = tails[k * PTAIL : (k + 1) * PTAIL, :]

    def gradients(gate, up, back):
        sig = jax.nn.sigmoid(gate)
        to_gate = back * up * sig * (1.0 + gate * (1.0 - sig))
        to_up = back * (gate * sig)
        return to_gate.T.astype(BF16), to_up.T.astype(BF16)

    depth = 512

    def forward(group):
        rows = pl.ds(group * PMAIN, PMAIN)
        tails = pl.ds(group * PTAIL, PTAIL)

        def one(step, total):
            columns = pl.ds(pl.multiple_of(step * depth, depth), depth)

            def side(kind):
                return [
                    wfull[q * PIECE + kind * SUB : q * PIECE + (kind + 1) * SUB, columns]
                    for q in range(SEG)
                ]

            gate_up = jnp.concatenate(side(0) + side(1), axis=0)
            down = jnp.concatenate(side(2), axis=0)
            tokens = jnp.concatenate([xbuf[0, rows, columns], xtail[0, tails, columns]], 0)
            scaled = jnp.concatenate([xbuf[1, rows, columns], xtail[1, tails, columns]], 0)
            return total[0] + nt_dot(tokens, gate_up), total[1] + nt_dot(scaled, down)

        count = PMAIN + PTAIL
        start = (jnp.zeros((count, 2 * WIDTH), F32), jnp.zeros((count, WIDTH), F32))
        front, back = lax.fori_loop(0, D // depth, one, start)
        to_gate, to_up = gradients(
            front[:PMAIN, :WIDTH], front[:PMAIN, WIDTH:], back[:PMAIN]
        )
        g_t[:WIDTH, rows] = to_gate
        g_t[WIDTH:, rows] = to_up
        pre_tail[tails, : 2 * WIDTH] = front[PMAIN:]
        pre_tail[tails, 2 * WIDTH :] = back[PMAIN:]

    weights_in(5)
    relay(2)
    unpack(0)
    weights_in(6)
    relay_far(2)
    unpack(1)
    weights_in(7)
    relay(3)
    unpack(2)
    weights_in(8)
    forward(0)
    relay_far(3)
    forward(1)
    forward(2)
    unpack(3)
    forward(3)
    to_gate, to_up = gradients(
        pre_tail[:, :WIDTH], pre_tail[:, WIDTH : 2 * WIDTH], pre_tail[:, 2 * WIDTH :]
    )
    g_t[:WIDTH, ROWS:] = to_gate
    g_t[WIDTH:, ROWS:] = to_up

    wide_out = 256

    def weight_gradient(turn):
        at = lax.rem(zl + turn, SEG)

        def one(step, carry):
            first = pl.multiple_of(at * QUART + step * wide_out, wide_out)
            total = dot(g_t[:, :ROWS], xbuf[0, :, pl.ds(first, wide_out)])
            total = total + dot(g_t[:, ROWS:], xtail[0, :, pl.ds(first, wide_out)])
            to = pl.ds(pl.multiple_of(step * wide_out, wide_out), wide_out)
            dw[at, :, to] = total
            return carry

        lax.fori_loop(0, QUART // wide_out, one, 0)

    def own_term(dest, kind):
        row = pl.multiple_of(kind * WIDTH + (dest // SEG) * SUB, SUB)
        return dw[lax.rem(dest, SEG), pl.ds(row, SUB), :]

    def sum_in(step, way, kind):
        ref = rs_in.at[way, step, kind]
        arrived(ref, r_s.at[way, step, kind], r_r.at[way, step, kind])
        return rs_in[way, step, kind].astype(F32)

    def sum_on(step):
        for kind in range(2):
            for way in range(2):
                if step == 0 and kind != way:
                    continue
                ahead = STEPS - step if way == 0 else NZ - STEPS + step
                total = own_term(lax.rem(z + ahead, NZ), kind)
                if step > 1 or (step == 1 and kind == way):
                    total = total + sum_in(step - 1, way, kind)
                rs_out[way, step, kind] = total.astype(BF16)
                send(
                    rs_out.at[way, step, kind],
                    rs_in.at[way, step, kind],
                    r_s.at[way, step, kind],
                    r_r.at[way, step, kind],
                    to_z[way],
                )

    weight_gradient(0)
    sum_on(0)
    weight_gradient(1)
    weight_gradient(3)
    sum_on(1)
    weight_gradient(2)
    for step in range(2, STEPS):
        sum_on(step)

    for kind in range(2):
        total = own_term(z, kind)
        for way in range(2):
            total = total + sum_in(STEPS - 1, way, kind)
        total = total.astype(BF16)
        for m in range(POOL):
            fin_out[m, kind * SUB : (kind + 1) * SUB, :] = total[
                :, m * FEAT : (m + 1) * FEAT
            ]
    own_sum = pltpu.make_async_copy(fin_out.at[p], fin_in.at[p], load_sem.at[4])
    own_sum.start()
    for k in range(1, POOL):
        to = lax.rem(p + k, POOL)
        send(fin_out.at[to], fin_in.at[p], f_s.at[k - 1], f_r.at[k - 1], member(to))
    own_sum.wait()
    for k in range(1, POOL):
        arrived(fin_in.at[lax.rem(p + POOL - k, POOL)], f_s.at[k - 1], f_r.at[k - 1])

    to_block = (iota((FEAT, FEAT), 0) // BLOCK == iota((FEAT, FEAT), 1)).astype(F32)
    for kind in range(2):
        summed = jnp.concatenate(
            [fin_in[m, kind * SUB : (kind + 1) * SUB, :] for m in range(POOL)], axis=0
        ).astype(F32)
        codes = gu_codes_ref[kind * HID : (kind + 1) * HID, :]
        grad_ref[kind * HID : (kind + 1) * HID, :] = jnp.where(codes % 8 != 7, summed, 0.0)
        blocks = jnp.dot(
            summed * decode_values(codes),
            to_block,
            precision=lax.Precision.HIGHEST,
            preferred_element_type=F32,
        )
        scale_ref[kind * HID : (kind + 1) * HID, :] = LSQ * blocks[:, : FEAT // BLOCK]
    for one in started:
        one.wait_send()


def body(tokens, cotangent, routes, combine, gu_codes, gu_scales, d_codes, d_scales):
    hidden, width = gu_codes.shape[1], gu_codes.shape[2]
    vmem = pl.BlockSpec(memory_space=pltpu.VMEM)
    hbm = pl.BlockSpec(memory_space=pl.ANY)
    dma = pltpu.SemaphoreType.DMA
    grad, scale = pl.pallas_call(
        kernel,
        out_shape=(
            jax.ShapeDtypeStruct((2 * hidden, width), F32),
            jax.ShapeDtypeStruct((2 * hidden, width // BLOCK), F32),
        ),
        in_specs=[hbm, hbm] + [vmem] * 6,
        out_specs=(vmem, vmem),
        scratch_shapes=[
            pltpu.VMEM((TOK, D), BF16),
            pltpu.VMEM((TOK, D), BF16),
            pltpu.VMEM((2, NX * MAIN, PACK), BF16),
            pltpu.VMEM((2, ROWS, PACK), BF16),
            pltpu.VMEM((2, TAILS, D), BF16),
            pltpu.VMEM((POOL, PIECE, FEAT), BF16),
            pltpu.VMEM((SEG * PIECE, D), BF16),
            pltpu.VMEM((TAILS, 3 * WIDTH), F32),
            pltpu.VMEM((2 * WIDTH, ROWS + TAILS), BF16),
            pltpu.VMEM((SEG, 2 * WIDTH, QUART), F32),
            pltpu.VMEM((2, STEPS, 2, SUB, QUART), BF16),
            pltpu.VMEM((2, STEPS, 2, SUB, QUART), BF16),
            pltpu.VMEM((POOL, 2 * SUB, FEAT), BF16),
            pltpu.VMEM((POOL, 2 * SUB, FEAT), BF16),
            dma((5,)),
            dma((NX - 1,)),
            dma((NX - 1,)),
            dma((2, 2, NX)),
            dma((2, 2, NX)),
            dma((NX, 5)),
            dma((NX, 5)),
            dma((POOL - 1,)),
            dma((POOL - 1,)),
            dma((2, STEPS)),
            dma((2, STEPS)),
            dma((2, STEPS, 2)),
            dma((2, STEPS, 2)),
            dma((POOL - 1,)),
            dma((POOL - 1,)),
        ],
        compiler_params=pltpu.CompilerParams(
            collective_id=0, has_side_effects=True, vmem_limit_bytes=56 << 20
        ),
        cost_estimate=pl.CostEstimate(
            flops=2 * 640 * D * 5 * WIDTH, bytes_accessed=8 << 20, transcendentals=0
        ),
    )(
        tokens,
        cotangent,
        routes.T,
        combine.T,
        gu_codes.reshape(2 * hidden, width),
        gu_scales.reshape(2 * hidden, width // BLOCK),
        d_codes,
        d_scales,
    )
    return (
        grad.reshape(2, hidden, width),
        scale.reshape(2, hidden, width // BLOCK),
    )


def solution(mesh):
    rows = P(("dp", "tensor"), None)
    return jax.shard_map(
        body,
        mesh=mesh,
        in_specs=(
            rows,
            rows,
            rows,
            rows,
            P(None, "tensor", "dp"),
            P(None, "tensor", "dp"),
            P("tensor", "dp"),
            P("tensor", "dp"),
        ),
        out_specs=(P(None, "tensor", "dp"), P(None, "tensor", "dp")),
        check_vma=False,
    )
```

```python
import jax
import jax.numpy as jnp
from jax import lax
from jax.experimental import pallas as pl
from jax.experimental.pallas import tpu as pltpu
from jax.sharding import PartitionSpec as P

BLOCK = 32
CAP = 20
NX, NY, NZ, NC = 4, 4, 16, 2
SEG = 4
POOL = NY * NC
D = 4096
TOK = 256
MAIN = 16
TAIL = CAP - MAIN
QUART = D // SEG
PACK = D + QUART
HID = 256
SUB = HID // POOL
FEAT = 128
PIECE = 3 * SUB
HALF = PIECE // 2
PMAIN = POOL * MAIN
PTAIL = POOL * TAIL
ROWS = NX * PMAIN
TAILS = NX * PTAIL
WIDTH = SEG * SUB
OFFSETS = (0, 1, 3, 2)
STEPS = NZ // 2
PART = QUART // NY
MESH = pl.DeviceIdType.MESH
LSQ = 192.0 ** (-0.5)
F32 = jnp.float32
BF16 = jnp.bfloat16


def decode_values(code_array):
    modulus = (code_array % 8).astype(F32)
    levels = jnp.where(
        modulus < 4.0,
        0.5 * modulus,
        jnp.where(modulus < 6.0, modulus - 2.0, jnp.where(modulus < 7.0, 4.0, 6.0)),
    )
    return jnp.where(code_array >= 8, -levels, levels)


def iota(shape, axis):
    return lax.broadcasted_iota(jnp.int32, shape, axis)


def nt_dot(a, b):
    return lax.dot_general(a, b, (((1,), (1,)), ((), ())), preferred_element_type=F32)


def dot(a, b):
    return jnp.dot(a, b, preferred_element_type=F32)


def device_at(x, y, z, c):
    return (y * (SEG * NC) + lax.rem(z, SEG) * NC + c, x * SEG + z // SEG)


def kernel(
    tok_hbm,
    cot_hbm,
    routes_hbm,
    combine_hbm,
    gu_codes_hbm,
    gu_scales_hbm,
    d_codes_hbm,
    d_scales_hbm,
    grad_ref,
    scale_ref,
    tok_v,
    cot_v,
    routes_ref,
    combine_ref,
    gu_codes_ref,
    gu_scales_ref,
    d_codes_ref,
    d_scales_ref,
    sbuf,
    xbuf,
    xtail,
    wsend,
    wfull,
    pre_tail,
    g_t,
    dw,
    rs_out,
    rs_in,
    fin_out,
    fin_in,
    load_sem,
    x_s,
    x_r,
    y_s,
    y_r,
    p_s,
    p_r,
    a_s,
    a_r,
    w_s,
    w_r,
    r_s,
    r_r,
    f_s,
    f_r,
):
    dp = lax.axis_index("dp")
    tensor = lax.axis_index("tensor")
    x, zh = tensor // SEG, lax.rem(tensor, SEG)
    y, rest = dp // (SEG * NC), lax.rem(dp, SEG * NC)
    zl, c = rest // NC, lax.rem(rest, NC)
    z = zh * SEG + zl
    p = y * NC + c
    oc = 1 - c
    y_up, y_dn, y_far = lax.rem(y + 1, NY), lax.rem(y + NY - 1, NY), lax.rem(y + 2, NY)
    z_up, z_dn = lax.rem(z + 1, NZ), lax.rem(z + NZ - 1, NZ)
    to_y = (device_at(x, y_up, z, c), device_at(x, y_dn, z, c))
    to_z = (device_at(x, y, z_up, c), device_at(x, y, z_dn, c))
    partner = device_at(x, y, z, oc)

    def member(index):
        return device_at(x, index // NC, z, lax.rem(index, NC))

    def copy(src, dst, sent, got, device):
        return pltpu.make_async_remote_copy(
            src_ref=src,
            dst_ref=dst,
            send_sem=sent,
            recv_sem=got,
            device_id=device,
            device_id_type=MESH,
        )

    started = []

    def send(src, dst, sent, got, device):
        one = copy(src, dst, sent, got, device)
        one.start()
        started.append(one)

    def arrived(dst, sent, got):
        copy(dst, dst, sent, got, partner).wait_recv()

    barrier = pltpu.get_barrier_semaphore()
    peers = [member(lax.rem(p + k, POOL)) for k in range(1, POOL)]
    peers += [device_at(lax.rem(x + o, NX), y, z, c) for o in range(1, NX)]
    peers += list(to_z)
    for peer in peers:
        pl.semaphore_signal(barrier, inc=1, device_id=peer, device_id_type=MESH)

    pairs = (
        (routes_hbm, routes_ref),
        (combine_hbm, combine_ref),
        (tok_hbm, tok_v),
        (gu_codes_hbm, gu_codes_ref),
        (gu_scales_hbm, gu_scales_ref),
        (d_codes_hbm, d_codes_ref),
        (d_scales_hbm, d_scales_ref),
        (cot_hbm, cot_v),
    )
    loads = [
        pltpu.make_async_copy(src, dst, load_sem.at[4 + i])
        for i, (src, dst) in enumerate(pairs)
    ]
    for one in loads:
        one.start()

    loads[0].wait()
    loads[1].wait()
    masks, weights = [], []
    for e in range(NX):
        chosen = routes_ref[...] == e
        masks.append(jnp.max(chosen.astype(F32), axis=0, keepdims=True))
        weights.append(
            jnp.sum(jnp.where(chosen, combine_ref[...], 0.0), axis=0, keepdims=True)
        )
    mask = jnp.concatenate(masks + [jnp.zeros((4, TOK), F32)], axis=0)
    before = (iota((TOK, TOK), 0) <= iota((TOK, TOK), 1)).astype(F32).astype(BF16)
    count = dot(mask.astype(BF16), before)
    place = jnp.where(mask > 0.0, count - 1.0, -1.0).astype(jnp.int32)
    wide = (MAIN, TOK)
    place = jnp.concatenate(
        [jnp.broadcast_to(place[e : e + 1], wide) for e in range(NX)], axis=0
    )
    weight = jnp.concatenate(
        [jnp.broadcast_to(weights[e], wide) for e in range(NX)], axis=0
    )
    slot = lax.rem(iota((NX * MAIN, TOK), 0), MAIN)
    is_main = place == slot
    is_tail = place == MAIN + lax.rem(slot, TAIL)
    main_weight = jnp.sum(jnp.where(is_main, weight, 0.0), axis=1, keepdims=True)
    tail_weight = jnp.sum(jnp.where(is_tail, weight, 0.0), axis=1, keepdims=True)
    pick_main = is_main.astype(F32).astype(BF16)
    picks = []
    for k in range(SEG):
        pick_tail = (is_tail & (slot // TAIL == k)).astype(F32).astype(BF16)
        picks.append(jnp.concatenate([pick_main, pick_tail], axis=0))

    def piece(origin, first=0, count=PIECE):
        row = pl.multiple_of((origin // SEG) * PIECE + first, 16)
        column = pl.multiple_of(lax.rem(origin, SEG) * QUART, QUART)
        return wfull.at[pl.ds(row, count), pl.ds(column, QUART)]

    def part(index):
        row = pl.multiple_of(zh * PIECE, 16)
        column = pl.multiple_of(zl * QUART + index * FEAT, FEAT)
        return wfull.at[pl.ds(row, PIECE), pl.ds(column, FEAT)]

    def for_expert(which, e):
        return sbuf.at[which, pl.ds(pl.multiple_of(e * MAIN, MAIN), MAIN), :]

    def rows_of(group, at_y, at_c):
        row = group * PMAIN + (at_y * NC + at_c) * MAIN
        return pl.ds(pl.multiple_of(row, MAIN), MAIN)

    def block(group, at_y, at_c):
        return xbuf.at[:, rows_of(group, at_y, at_c), :]

    def one_block(which, group, at_y, at_c):
        return xbuf.at[which, rows_of(group, at_y, at_c), :]

    def own_part_of(which, group):
        return one_block(which, group, y, c)

    def spread(which, group):
        if group == 0:
            source = for_expert(which, x)
        else:
            source = own_part_of(which, group)
            arrived(source, x_s.at[which, group - 1], x_r.at[which, group - 1])
        for way in range(2):
            send(
                source,
                own_part_of(which, group),
                y_s.at[which, way, group],
                y_r.at[which, way, group],
                to_y[way],
            )
        sems = p_s.at[group, 5 * which], p_r.at[group, 5 * which]
        send(source, own_part_of(which, group), *sems, partner)

    for one in loads[3:7]:
        one.wait()
    lane_block = iota((HID, FEAT), 1) // BLOCK
    for g in range(2):
        rows = pl.ds(g * HID, HID)
        padding = jnp.zeros((FEAT - FEAT // BLOCK, HID), F32)
        turned = jnp.concatenate([gu_scales_ref[g], padding], axis=0).T
        scale = jnp.zeros((HID, FEAT), F32)
        for b in range(FEAT // BLOCK):
            scale = jnp.where(lane_block == b, turned[:, b : b + 1], scale)
        weight = (scale * decode_values(gu_codes_ref[rows, :])).astype(BF16)
        for m in range(POOL):
            wsend[m, g * SUB : (g + 1) * SUB, :] = weight[m * SUB : (m + 1) * SUB, :]
    for m in range(POOL):
        values = decode_values(d_codes_ref[m * SUB : (m + 1) * SUB, :])
        wsend[m, 2 * SUB : 3 * SUB, :] = (d_scales_ref[m : m + 1, :] * values).astype(BF16)

    wide = QUART // NY
    own_rows = []
    for which, (source, load) in enumerate(((tok_v, loads[2]), (cot_v, loads[7]))):
        load.wait()
        for quarter in range(NY):
            folded = jnp.zeros((NX * MAIN, wide), F32)
            for k in range(SEG):
                first = quarter * QUART + k * wide
                both = dot(picks[k], source[:, first : first + wide])
                picked = both[: NX * MAIN]
                folded = folded + both[NX * MAIN :]
                if which == 1:
                    picked = picked * main_weight
                to = k * QUART + quarter * wide
                sbuf[which, :, to : to + wide] = picked.astype(BF16)
            if which == 1:
                folded = folded * tail_weight
            to = D + quarter * wide
            sbuf[which, :, to : to + wide] = folded.astype(BF16)
        if which == 0:
            pl.semaphore_wait(barrier, len(peers))
            own_part = pltpu.make_async_copy(wsend.at[p], part(p), load_sem.at[2])
            own_part.start()
            for k in range(1, POOL):
                to = lax.rem(p + k, POOL)
                send(wsend.at[to], part(p), a_s.at[k - 1], a_r.at[k - 1], member(to))
        for group in range(1, NX):
            e = lax.rem(x + OFFSETS[group], NX)
            send(
                for_expert(which, e),
                own_part_of(which, group),
                x_s.at[which, group - 1],
                x_r.at[which, group - 1],
                device_at(e, y, z, c),
            )
        spread(which, 0)
        own_rows.append(
            pltpu.make_async_copy(
                for_expert(which, x), own_part_of(which, 0), load_sem.at[which]
            )
        )
        own_rows[which].start()

    def relay(group):
        for way in range(2):
            from_y = (y_dn, y_up)[way]
            whole = block(group, from_y, c)
            for which in range(2):
                half = one_block(which, group, from_y, c)
                arrived(half, y_s.at[which, way, group], y_r.at[which, way, group])
            half = one_block(way, group, from_y, c)
            send(half, half, y_s.at[2, way, group], y_r.at[2, way, group], to_y[way])
            send(whole, whole, p_s.at[group, 1 + way], p_r.at[group, 1 + way], partner)

    def relay_far(group):
        for way in range(2):
            half = one_block(way, group, y_far, c)
            arrived(half, y_s.at[2, way, group], y_r.at[2, way, group])
            send(half, half, p_s.at[group, 3 + way], p_r.at[group, 3 + way], partner)

    def all_rows(group):
        for which in range(2):
            half = one_block(which, group, y, oc)
            arrived(half, p_s.at[group, 5 * which], p_r.at[group, 5 * which])
        arrived(block(group, y_dn, oc), p_s.at[group, 1], p_r.at[group, 1])
        arrived(block(group, y_up, oc), p_s.at[group, 2], p_r.at[group, 2])
        for way in range(2):
            half = one_block(way, group, y_far, oc)
            arrived(half, p_s.at[group, 3 + way], p_r.at[group, 3 + way])

    def ways_of(step, half):
        return range(2) if step < STEPS else (half,)

    def weights_on(step, half):
        for way in ways_of(step, half):
            back = NZ - (step - 1) if way == 0 else step - 1
            ref = piece(lax.rem(z + back, NZ), half * HALF, HALF)
            sems = w_s.at[way, step - 1, half], w_r.at[way, step - 1, half]
            send(ref, ref, *sems, to_z[way])

    def weights_in(step, half):
        for way in ways_of(step, half):
            back = NZ - step if way == 0 else step
            ref = piece(lax.rem(z + back, NZ), half * HALF, HALF)
            arrived(ref, w_s.at[way, step - 1, half], w_r.at[way, step - 1, half])
        if step < STEPS:
            weights_on(step + 1, half)

    fold_from = iota((PMAIN, PMAIN), 1)
    fold_to = iota((PMAIN, PMAIN), 0)
    inside = lax.rem(fold_to, PTAIL)
    wanted = (inside // TAIL) * MAIN + (fold_to // PTAIL) * TAIL + lax.rem(inside, TAIL)
    unfold = (fold_from == wanted).astype(F32).astype(BF16)

    def unpack(group):
        all_rows(group)
        for which in range(2):
            folded = xbuf[which, group * PMAIN : (group + 1) * PMAIN, D:PACK]
            tails = dot(unfold, folded).astype(BF16)
            for k in range(SEG):
                xtail[
                    which,
                    group * PTAIL : (group + 1) * PTAIL,
                    k * QUART : (k + 1) * QUART,
                ] = tails[k * PTAIL : (k + 1) * PTAIL, :]

    def gradients(gate, up, back):
        sig = jax.nn.sigmoid(gate)
        to_gate = back * up * sig * (1.0 + gate * (1.0 - sig))
        to_up = back * (gate * sig)
        return to_gate.T.astype(BF16), to_up.T.astype(BF16)

    depth = 2048

    def forward(group):
        rows = pl.ds(group * PMAIN, PMAIN)
        tails = pl.ds(group * PTAIL, PTAIL)

        def one(step, total):
            columns = pl.ds(pl.multiple_of(step * depth, depth), depth)

            def side(kind):
                return [
                    wfull[q * PIECE + kind * SUB : q * PIECE + (kind + 1) * SUB, columns]
                    for q in range(SEG)
                ]

            gate_up = jnp.concatenate(side(0) + side(1), axis=0)
            down = jnp.concatenate(side(2), axis=0)
            tokens = jnp.concatenate([xbuf[0, rows, columns], xtail[0, tails, columns]], 0)
            scaled = jnp.concatenate([xbuf[1, rows, columns], xtail[1, tails, columns]], 0)
            return total[0] + nt_dot(tokens, gate_up), total[1] + nt_dot(scaled, down)

        count = PMAIN + PTAIL
        start = (jnp.zeros((count, 2 * WIDTH), F32), jnp.zeros((count, WIDTH), F32))
        front, back = lax.fori_loop(0, D // depth, one, start)
        to_gate, to_up = gradients(
            front[:PMAIN, :WIDTH], front[:PMAIN, WIDTH:], back[:PMAIN]
        )
        g_t[:WIDTH, rows] = to_gate
        g_t[WIDTH:, rows] = to_up
        pre_tail[tails, : 2 * WIDTH] = front[PMAIN:]
        pre_tail[tails, 2 * WIDTH :] = back[PMAIN:]

    own_part.wait()
    for k in range(1, POOL):
        got = part(lax.rem(p + POOL - k, POOL))
        arrived(got, a_s.at[k - 1], a_r.at[k - 1])
    weights_on(1, 0)
    weights_on(1, 1)

    weights_in(1, 0)
    spread(0, 1)
    spread(0, 2)
    weights_in(1, 1)
    relay(0)
    spread(0, 3)
    weights_in(2, 0)
    weights_in(2, 1)
    spread(1, 1)
    spread(1, 2)
    weights_in(3, 0)
    weights_in(3, 1)
    spread(1, 3)
    weights_in(4, 0)
    weights_in(4, 1)
    for one in own_rows:
        one.wait()
    weights_in(5, 0)
    weights_in(5, 1)
    weights_in(6, 0)
    weights_in(6, 1)
    relay(1)
    weights_in(7, 0)
    relay_far(0)
    weights_in(7, 1)
    relay(2)
    weights_in(8, 0)
    weights_in(8, 1)
    relay(3)
    unpack(0)
    forward(0)
    relay_far(1)
    unpack(1)
    forward(1)
    relay_far(2)
    unpack(2)
    forward(2)
    relay_far(3)
    unpack(3)
    forward(3)
    to_gate, to_up = gradients(
        pre_tail[:, :WIDTH], pre_tail[:, WIDTH : 2 * WIDTH], pre_tail[:, 2 * WIDTH :]
    )
    g_t[:WIDTH, ROWS:] = to_gate
    g_t[WIDTH:, ROWS:] = to_up

    def turn_y(turn):
        return lax.rem(y + 1 + turn, NY)

    def columns_of(turn):
        return pl.ds(pl.multiple_of(turn_y(turn) * PART, PART), PART)

    def weight_gradient(ahead, turn):
        at = lax.rem(zl + ahead, SEG)
        first = pl.multiple_of(at * QUART + turn_y(turn) * PART, PART)
        total = dot(g_t[:, :ROWS], xbuf[0, :, pl.ds(first, PART)])
        total = total + dot(g_t[:, ROWS:], xtail[0, :, pl.ds(first, PART)])
        dw[at, :, columns_of(turn)] = total

    def own_term(dest, kind, turn):
        row = pl.multiple_of(kind * WIDTH + (dest // SEG) * SUB, SUB)
        return dw[lax.rem(dest, SEG), pl.ds(row, SUB), columns_of(turn)]

    def sum_part(ref, step, way, turn):
        if step == 0:
            return ref.at[way, step, turn, way * SUB : (way + 1) * SUB, :]
        return ref.at[way, step, turn]

    def sum_in(step, way, turn):
        ref = sum_part(rs_in, step, way, turn)
        arrived(ref, r_s.at[way, step, turn], r_r.at[way, step, turn])

    def came(step, way, turn, kind):
        return rs_in[way, step, turn, kind * SUB : (kind + 1) * SUB, :].astype(F32)

    def sum_on(step, turn):
        for way in range(2):
            if step > 0:
                sum_in(step - 1, way, turn)
            ahead = STEPS - step if way == 0 else NZ - STEPS + step
            for kind in range(2):
                if step == 0 and kind != way:
                    continue
                total = own_term(lax.rem(z + ahead, NZ), kind, turn)
                if step > 1 or (step == 1 and kind == way):
                    total = total + came(step - 1, way, turn, kind)
                rows = slice(kind * SUB, (kind + 1) * SUB)
                rs_out[way, step, turn, rows, :] = total.astype(BF16)
            send(
                sum_part(rs_out, step, way, turn),
                sum_part(rs_in, step, way, turn),
                r_s.at[way, step, turn],
                r_r.at[way, step, turn],
                to_z[way],
            )

    own_sum = pltpu.make_async_copy(fin_out.at[p], fin_in.at[p], load_sem.at[3])

    def sum_out(turn):
        for way in range(2):
            sum_in(STEPS - 1, way, turn)
        to_y_here = turn_y(turn)
        for kind in range(2):
            total = own_term(z, kind, turn)
            for way in range(2):
                total = total + came(STEPS - 1, way, turn, kind)
            total = total.astype(BF16)
            for core in range(NC):
                fin_out[to_y_here * NC + core, kind * SUB : (kind + 1) * SUB, :] = total[
                    :, core * FEAT : (core + 1) * FEAT
                ]
        for other in range(NC):
            if turn == NY - 1 and other == 0:
                own_sum.start()
                continue
            to = to_y_here * NC + lax.rem(c + other, NC)
            sems = f_s.at[turn, other], f_r.at[turn, other]
            send(fin_out.at[to], fin_in.at[p], *sems, member(to))

    for turn in range(NY):
        weight_gradient(0, turn)
        sum_on(0, turn)
    for turn in range(NY):
        weight_gradient(1, turn)
        weight_gradient(3, turn)
        sum_on(1, turn)
    for turn in range(NY):
        weight_gradient(2, turn)
        sum_on(2, turn)
    for step in range(3, STEPS):
        for turn in range(NY):
            sum_on(step, turn)
    for turn in range(NY):
        sum_out(turn)
    for one in started:
        one.wait_send()
    own_sum.wait()
    for turn in range(NY):
        for other in range(NC):
            if turn == NY - 1 and other == 0:
                continue
            origin = lax.rem(y + NY - 1 - turn, NY) * NC + lax.rem(c + other, NC)
            arrived(fin_in.at[origin], f_s.at[turn, other], f_r.at[turn, other])

    to_block = (iota((8, FEAT), 1) // BLOCK == iota((8, FEAT), 0)).astype(F32)
    for kind in range(2):
        summed = jnp.concatenate(
            [fin_in[m, kind * SUB : (kind + 1) * SUB, :] for m in range(POOL)], axis=0
        ).astype(F32)
        codes = gu_codes_ref[kind * HID : (kind + 1) * HID, :]
        grad_ref[kind * HID : (kind + 1) * HID, :] = jnp.where(codes % 8 != 7, summed, 0.0)
        blocks = lax.dot_general(
            to_block,
            summed * decode_values(codes),
            (((1,), (1,)), ((), ())),
            precision=lax.Precision.HIGHEST,
            preferred_element_type=F32,
        )
        scale_ref[kind] = LSQ * blocks[: FEAT // BLOCK]


def body(tokens, cotangent, routes, combine, gu_codes, gu_scales, d_codes, d_scales):
    hidden, width = gu_codes.shape[1], gu_codes.shape[2]
    vmem = pl.BlockSpec(memory_space=pltpu.VMEM)
    hbm = pl.BlockSpec(memory_space=pl.ANY)
    dma = pltpu.SemaphoreType.DMA
    grad, scale = pl.pallas_call(
        kernel,
        out_shape=(
            jax.ShapeDtypeStruct((2 * hidden, width), F32),
            jax.ShapeDtypeStruct((2, width // BLOCK, hidden), F32),
        ),
        in_specs=[hbm] * 8,
        out_specs=(vmem, vmem),
        scratch_shapes=[
            pltpu.VMEM((TOK, D), BF16),
            pltpu.VMEM((TOK, D), BF16),
            pltpu.VMEM(routes.shape[::-1], jnp.int32),
            pltpu.VMEM(combine.shape[::-1], F32),
            pltpu.VMEM((2 * hidden, width), jnp.int32),
            pltpu.VMEM((2, width // BLOCK, hidden), F32),
            pltpu.VMEM(d_codes.shape, jnp.int32),
            pltpu.VMEM(d_scales.shape, F32),
            pltpu.VMEM((2, NX * MAIN, PACK), BF16),
            pltpu.VMEM((2, ROWS, PACK), BF16),
            pltpu.VMEM((2, TAILS, D), BF16),
            pltpu.VMEM((POOL, PIECE, FEAT), BF16),
            pltpu.VMEM((SEG * PIECE, D), BF16),
            pltpu.VMEM((TAILS, 3 * WIDTH), F32),
            pltpu.VMEM((2 * WIDTH, ROWS + TAILS), BF16),
            pltpu.VMEM((SEG, 2 * WIDTH, QUART), F32),
            pltpu.VMEM((2, STEPS, NY, 2 * SUB, PART), BF16),
            pltpu.VMEM((2, STEPS, NY, 2 * SUB, PART), BF16),
            pltpu.VMEM((POOL, 2 * SUB, FEAT), BF16),
            pltpu.VMEM((POOL, 2 * SUB, FEAT), BF16),
            dma((12,)),
            dma((2, NX - 1)),
            dma((2, NX - 1)),
            dma((3, 2, NX)),
            dma((3, 2, NX)),
            dma((NX, 6)),
            dma((NX, 6)),
            dma((POOL - 1,)),
            dma((POOL - 1,)),
            dma((2, STEPS, 2)),
            dma((2, STEPS, 2)),
            dma((2, STEPS, NY)),
            dma((2, STEPS, NY)),
            dma((NY, NC)),
            dma((NY, NC)),
        ],
        compiler_params=pltpu.CompilerParams(
            collective_id=0, has_side_effects=True, vmem_limit_bytes=56 << 20
        ),
        cost_estimate=pl.CostEstimate(
            flops=2 * 640 * D * 5 * WIDTH, bytes_accessed=8 << 20, transcendentals=0
        ),
    )(
        tokens,
        cotangent,
        routes.T,
        combine.T,
        gu_codes.reshape(2 * hidden, width),
        gu_scales.swapaxes(1, 2),
        d_codes,
        d_scales,
    )
    return (
        grad.reshape(2, hidden, width),
        scale.swapaxes(1, 2),
    )


def solution(mesh):
    rows = P(("dp", "tensor"), None)
    return jax.shard_map(
        body,
        mesh=mesh,
        in_specs=(
            rows,
            rows,
            rows,
            rows,
            P(None, "tensor", "dp"),
            P(None, "tensor", "dp"),
            P("tensor", "dp"),
            P("tensor", "dp"),
        ),
        out_specs=(P(None, "tensor", "dp"), P(None, "tensor", "dp")),
        check_vma=False,
    )
```

```python
import jax
import jax.numpy as jnp
from jax import lax
from jax.experimental import pallas as pl
from jax.experimental.pallas import tpu as pltpu
from jax.sharding import PartitionSpec as P

BLOCK = 32
CAP = 20
NX, NY, NZ, NC = 4, 4, 16, 2
SEG = 4
POOL = NY * NC
D = 4096
TOK = 256
MAIN = 16
TAIL = CAP - MAIN
QUART = D // SEG
PACK = D + QUART
HID = 256
SUB = HID // POOL
FEAT = 128
PIECE = 3 * SUB
HALF = PIECE // 2
PMAIN = POOL * MAIN
PTAIL = POOL * TAIL
ROWS = NX * PMAIN
TAILS = NX * PTAIL
WIDTH = SEG * SUB
OFFSETS = (0, 1, 3, 2)
STEPS = NZ // 2
PART = QUART // NY
MESH = pl.DeviceIdType.MESH
LSQ = 192.0 ** (-0.5)
F32 = jnp.float32
BF16 = jnp.bfloat16


def decode_values(code_array):
    modulus = (code_array % 8).astype(F32)
    levels = jnp.where(
        modulus < 4.0,
        0.5 * modulus,
        jnp.where(modulus < 6.0, modulus - 2.0, jnp.where(modulus < 7.0, 4.0, 6.0)),
    )
    return jnp.where(code_array >= 8, -levels, levels)


def iota(shape, axis):
    return lax.broadcasted_iota(jnp.int32, shape, axis)


def nt_dot(a, b):
    return lax.dot_general(a, b, (((1,), (1,)), ((), ())), preferred_element_type=F32)


def dot(a, b):
    return jnp.dot(a, b, preferred_element_type=F32)


def device_at(x, y, z, c):
    return (y * (SEG * NC) + lax.rem(z, SEG) * NC + c, x * SEG + z // SEG)


def kernel(
    tok_hbm,
    cot_hbm,
    routes_hbm,
    combine_hbm,
    gu_codes_hbm,
    gu_scales_hbm,
    d_codes_hbm,
    d_scales_hbm,
    fin_in,
    tok_v,
    cot_v,
    routes_ref,
    combine_ref,
    gu_codes_ref,
    gu_scales_ref,
    d_codes_ref,
    d_scales_ref,
    sbuf,
    xbuf,
    xtail,
    wsend,
    wfull,
    pre,
    pre_tail,
    g_t,
    dw,
    rs_out,
    rs_in,
    fin_out,
    load_sem,
    x_s,
    x_r,
    y_s,
    y_r,
    p_s,
    p_r,
    a_s,
    a_r,
    w_s,
    w_r,
    r_s,
    r_r,
    f_s,
    f_r,
):
    dp = lax.axis_index("dp")
    tensor = lax.axis_index("tensor")
    x, zh = tensor // SEG, lax.rem(tensor, SEG)
    y, rest = dp // (SEG * NC), lax.rem(dp, SEG * NC)
    zl, c = rest // NC, lax.rem(rest, NC)
    z = zh * SEG + zl
    p = y * NC + c
    oc = 1 - c
    y_up, y_dn, y_far = lax.rem(y + 1, NY), lax.rem(y + NY - 1, NY), lax.rem(y + 2, NY)
    z_up, z_dn = lax.rem(z + 1, NZ), lax.rem(z + NZ - 1, NZ)
    to_y = (device_at(x, y_up, z, c), device_at(x, y_dn, z, c))
    to_z = (device_at(x, y, z_up, c), device_at(x, y, z_dn, c))
    over_z = (
        device_at(x, y, lax.rem(z + 2, NZ), c),
        device_at(x, y, lax.rem(z + NZ - 2, NZ), c),
    )
    partner = device_at(x, y, z, oc)

    def member(index):
        return device_at(x, index // NC, z, lax.rem(index, NC))

    def copy(src, dst, sent, got, device):
        return pltpu.make_async_remote_copy(
            src_ref=src,
            dst_ref=dst,
            send_sem=sent,
            recv_sem=got,
            device_id=device,
            device_id_type=MESH,
        )

    started = []

    def send(src, dst, sent, got, device):
        one = copy(src, dst, sent, got, device)
        one.start()
        started.append(one)

    def arrived(dst, sent, got):
        copy(dst, dst, sent, got, partner).wait_recv()

    barrier = pltpu.get_barrier_semaphore()
    peers = [member(lax.rem(p + k, POOL)) for k in range(1, POOL)]
    peers += [device_at(lax.rem(x + o, NX), y, z, c) for o in range(1, NX)]
    peers += list(to_z) + list(over_z)
    for peer in peers:
        pl.semaphore_signal(barrier, inc=1, device_id=peer, device_id_type=MESH)

    pairs = (
        (routes_hbm, routes_ref),
        (combine_hbm, combine_ref),
        (tok_hbm, tok_v),
        (gu_codes_hbm, gu_codes_ref),
        (gu_scales_hbm, gu_scales_ref),
        (d_codes_hbm, d_codes_ref),
        (d_scales_hbm, d_scales_ref),
        (cot_hbm, cot_v),
    )
    loads = [
        pltpu.make_async_copy(src, dst, load_sem.at[4 + i])
        for i, (src, dst) in enumerate(pairs)
    ]
    for one in loads:
        one.start()

    loads[0].wait()
    loads[1].wait()
    masks, weights = [], []
    for e in range(NX):
        chosen = routes_ref[...] == e
        masks.append(jnp.max(chosen.astype(F32), axis=0, keepdims=True))
        weights.append(
            jnp.sum(jnp.where(chosen, combine_ref[...], 0.0), axis=0, keepdims=True)
        )
    mask = jnp.concatenate(masks + [jnp.zeros((4, TOK), F32)], axis=0)
    before = (iota((TOK, TOK), 0) <= iota((TOK, TOK), 1)).astype(F32).astype(BF16)
    count = dot(mask.astype(BF16), before)
    place = jnp.where(mask > 0.0, count - 1.0, -1.0).astype(jnp.int32)
    wide = (MAIN, TOK)
    place = jnp.concatenate(
        [jnp.broadcast_to(place[e : e + 1], wide) for e in range(NX)], axis=0
    )
    weight = jnp.concatenate(
        [jnp.broadcast_to(weights[e], wide) for e in range(NX)], axis=0
    )
    slot = lax.rem(iota((NX * MAIN, TOK), 0), MAIN)
    is_main = place == slot
    is_tail = place == MAIN + lax.rem(slot, TAIL)
    main_weight = jnp.sum(jnp.where(is_main, weight, 0.0), axis=1, keepdims=True)
    tail_weight = jnp.sum(jnp.where(is_tail, weight, 0.0), axis=1, keepdims=True)
    pick_main = is_main.astype(F32).astype(BF16)
    picks = []
    for k in range(SEG):
        pick_tail = (is_tail & (slot // TAIL == k)).astype(F32).astype(BF16)
        picks.append(jnp.concatenate([pick_main, pick_tail], axis=0))

    def piece(origin, first=0, count=PIECE):
        row = pl.multiple_of((origin // SEG) * PIECE + first, 16)
        column = pl.multiple_of(lax.rem(origin, SEG) * QUART, QUART)
        return wfull.at[pl.ds(row, count), pl.ds(column, QUART)]

    def part(index):
        row = pl.multiple_of(zh * PIECE, 16)
        column = pl.multiple_of(zl * QUART + index * FEAT, FEAT)
        return wfull.at[pl.ds(row, PIECE), pl.ds(column, FEAT)]

    def for_expert(which, e):
        return sbuf.at[which, pl.ds(pl.multiple_of(e * MAIN, MAIN), MAIN), :]

    def rows_of(group, at_y, at_c):
        row = group * PMAIN + (at_y * NC + at_c) * MAIN
        return pl.ds(pl.multiple_of(row, MAIN), MAIN)

    def block(group, at_y, at_c):
        return xbuf.at[:, rows_of(group, at_y, at_c), :]

    def one_block(which, group, at_y, at_c):
        return xbuf.at[which, rows_of(group, at_y, at_c), :]

    def own_part_of(which, group):
        return one_block(which, group, y, c)

    def spread(which, group):
        if group == 0:
            source = for_expert(which, x)
        else:
            source = own_part_of(which, group)
            arrived(source, x_s.at[which, group - 1], x_r.at[which, group - 1])
        for way in range(2):
            send(
                source,
                own_part_of(which, group),
                y_s.at[which, way, group],
                y_r.at[which, way, group],
                to_y[way],
            )
        sems = p_s.at[group, 5 * which], p_r.at[group, 5 * which]
        send(source, own_part_of(which, group), *sems, partner)

    for one in loads[3:7]:
        one.wait()
    lane_block = iota((HID, FEAT), 1) // BLOCK
    for g in range(2):
        rows = pl.ds(g * HID, HID)
        padding = jnp.zeros((FEAT - FEAT // BLOCK, HID), F32)
        turned = jnp.concatenate([gu_scales_ref[g], padding], axis=0).T
        scale = jnp.zeros((HID, FEAT), F32)
        for b in range(FEAT // BLOCK):
            scale = jnp.where(lane_block == b, turned[:, b : b + 1], scale)
        weight = (scale * decode_values(gu_codes_ref[rows, :])).astype(BF16)
        for m in range(POOL):
            wsend[m, g * SUB : (g + 1) * SUB, :] = weight[m * SUB : (m + 1) * SUB, :]
    for m in range(POOL):
        values = decode_values(d_codes_ref[m * SUB : (m + 1) * SUB, :])
        wsend[m, 2 * SUB : 3 * SUB, :] = (d_scales_ref[m : m + 1, :] * values).astype(BF16)

    wide = QUART // NY
    own_rows = []
    for which, (source, load) in enumerate(((tok_v, loads[2]), (cot_v, loads[7]))):
        load.wait()
        for quarter in range(NY):
            folded = jnp.zeros((NX * MAIN, wide), F32)
            for k in range(SEG):
                first = quarter * QUART + k * wide
                both = dot(picks[k], source[:, first : first + wide])
                picked = both[: NX * MAIN]
                folded = folded + both[NX * MAIN :]
                if which == 1:
                    picked = picked * main_weight
                to = k * QUART + quarter * wide
                sbuf[which, :, to : to + wide] = picked.astype(BF16)
            if which == 1:
                folded = folded * tail_weight
            to = D + quarter * wide
            sbuf[which, :, to : to + wide] = folded.astype(BF16)
        if which == 0:
            pl.semaphore_wait(barrier, len(peers))
            own_part = pltpu.make_async_copy(wsend.at[p], part(p), load_sem.at[2])
            own_part.start()
            for k in range(1, POOL):
                to = lax.rem(p + k, POOL)
                send(wsend.at[to], part(p), a_s.at[k - 1], a_r.at[k - 1], member(to))
        for group in range(1, NX):
            e = lax.rem(x + OFFSETS[group], NX)
            send(
                for_expert(which, e),
                own_part_of(which, group),
                x_s.at[which, group - 1],
                x_r.at[which, group - 1],
                device_at(e, y, z, c),
            )
        spread(which, 0)
        own_rows.append(
            pltpu.make_async_copy(
                for_expert(which, x), own_part_of(which, 0), load_sem.at[which]
            )
        )
        own_rows[which].start()

    def relay(group):
        for way in range(2):
            from_y = (y_dn, y_up)[way]
            whole = block(group, from_y, c)
            for which in range(2):
                half = one_block(which, group, from_y, c)
                arrived(half, y_s.at[which, way, group], y_r.at[which, way, group])
            half = one_block(way, group, from_y, c)
            send(half, half, y_s.at[2, way, group], y_r.at[2, way, group], to_y[way])
            send(whole, whole, p_s.at[group, 1 + way], p_r.at[group, 1 + way], partner)

    def relay_far(group):
        for way in range(2):
            half = one_block(way, group, y_far, c)
            arrived(half, y_s.at[2, way, group], y_r.at[2, way, group])
            send(half, half, p_s.at[group, 3 + way], p_r.at[group, 3 + way], partner)

    def all_rows(group):
        for which in range(2):
            half = one_block(which, group, y, oc)
            arrived(half, p_s.at[group, 5 * which], p_r.at[group, 5 * which])
        arrived(block(group, y_dn, oc), p_s.at[group, 1], p_r.at[group, 1])
        arrived(block(group, y_up, oc), p_s.at[group, 2], p_r.at[group, 2])
        for way in range(2):
            half = one_block(way, group, y_far, oc)
            arrived(half, p_s.at[group, 3 + way], p_r.at[group, 3 + way])

    def ways_of(step, half):
        return range(2) if step < STEPS else (half,)

    def weights_on(step, half):
        for way in ways_of(step, half):
            back = NZ - (step - 1) if way == 0 else step - 1
            ref = piece(lax.rem(z + back, NZ), half * HALF, HALF)
            sems = w_s.at[way, step - 1, half], w_r.at[way, step - 1, half]
            send(ref, ref, *sems, to_z[way])

    def weights_in(step, half):
        for way in ways_of(step, half):
            back = NZ - step if way == 0 else step
            ref = piece(lax.rem(z + back, NZ), half * HALF, HALF)
            arrived(ref, w_s.at[way, step - 1, half], w_r.at[way, step - 1, half])
        if step < STEPS:
            weights_on(step + 1, half)

    fold_from = iota((PMAIN, PMAIN), 1)
    fold_to = iota((PMAIN, PMAIN), 0)
    inside = lax.rem(fold_to, PTAIL)
    wanted = (inside // TAIL) * MAIN + (fold_to // PTAIL) * TAIL + lax.rem(inside, TAIL)
    unfold = (fold_from == wanted).astype(F32).astype(BF16)

    def unpack(group):
        all_rows(group)
        for which in range(2):
            folded = xbuf[which, group * PMAIN : (group + 1) * PMAIN, D:PACK]
            tails = dot(unfold, folded).astype(BF16)
            for k in range(SEG):
                xtail[
                    which,
                    group * PTAIL : (group + 1) * PTAIL,
                    k * QUART : (k + 1) * QUART,
                ] = tails[k * PTAIL : (k + 1) * PTAIL, :]

    def gradients(gate, up, back):
        sig = jax.nn.sigmoid(gate)
        to_gate = back * up * sig * (1.0 + gate * (1.0 - sig))
        to_up = back * (gate * sig)
        return to_gate.T.astype(BF16), to_up.T.astype(BF16)

    def forward(group, quarters, first, last):
        rows = pl.ds(group * PMAIN, PMAIN)
        tails = pl.ds(group * PTAIL, PTAIL)
        count = PMAIN + PTAIL
        if first:
            front = jnp.zeros((count, 2 * WIDTH), F32)
            back = jnp.zeros((count, WIDTH), F32)
        else:
            front, back = pre[group, :, : 2 * WIDTH], pre[group, :, 2 * WIDTH :]
        for quarter in quarters:
            at = pl.multiple_of(lax.rem(zl + quarter, SEG) * QUART, QUART)
            columns = pl.ds(at, QUART)

            def side(kind):
                return [
                    wfull[q * PIECE + kind * SUB : q * PIECE + (kind + 1) * SUB, columns]
                    for q in range(SEG)
                ]

            gate_up = jnp.concatenate(side(0) + side(1), axis=0)
            down = jnp.concatenate(side(2), axis=0)
            tokens = jnp.concatenate([xbuf[0, rows, columns], xtail[0, tails, columns]], 0)
            scaled = jnp.concatenate([xbuf[1, rows, columns], xtail[1, tails, columns]], 0)
            front = front + nt_dot(tokens, gate_up)
            back = back + nt_dot(scaled, down)
        if not last:
            pre[group, :, : 2 * WIDTH] = front
            pre[group, :, 2 * WIDTH :] = back
            return
        to_gate, to_up = gradients(
            front[:PMAIN, :WIDTH], front[:PMAIN, WIDTH:], back[:PMAIN]
        )
        g_t[:WIDTH, rows] = to_gate
        g_t[WIDTH:, rows] = to_up
        pre_tail[tails, : 2 * WIDTH] = front[PMAIN:]
        pre_tail[tails, 2 * WIDTH :] = back[PMAIN:]

    own_part.wait()
    for k in range(1, POOL):
        got = part(lax.rem(p + POOL - k, POOL))
        arrived(got, a_s.at[k - 1], a_r.at[k - 1])
    weights_on(1, 0)
    weights_on(1, 1)

    weights_in(1, 0)
    spread(0, 1)
    spread(0, 2)
    weights_in(1, 1)
    relay(0)
    spread(0, 3)
    weights_in(2, 0)
    weights_in(2, 1)
    spread(1, 1)
    spread(1, 2)
    weights_in(3, 0)
    weights_in(3, 1)
    spread(1, 3)
    weights_in(4, 0)
    weights_in(4, 1)
    for one in own_rows:
        one.wait()
    weights_in(5, 0)
    weights_in(5, 1)
    relay(1)
    weights_in(6, 0)
    relay_far(0)
    weights_in(6, 1)
    relay(2)
    unpack(0)
    forward(0, (2,), True, False)
    weights_in(7, 0)
    weights_in(7, 1)
    forward(0, (1, 3), False, False)
    relay(3)
    relay_far(1)
    unpack(1)
    forward(1, (2, 1, 3), True, False)
    relay_far(2)
    unpack(2)
    forward(2, (2, 1, 3), True, False)
    weights_in(8, 0)
    weights_in(8, 1)
    forward(0, (0,), False, True)
    forward(1, (0,), False, True)
    forward(2, (0,), False, True)
    relay_far(3)
    unpack(3)
    forward(3, (0, 1, 2, 3), True, True)
    to_gate, to_up = gradients(
        pre_tail[:, :WIDTH], pre_tail[:, WIDTH : 2 * WIDTH], pre_tail[:, 2 * WIDTH :]
    )
    g_t[:WIDTH, ROWS:] = to_gate
    g_t[WIDTH:, ROWS:] = to_up

    def turn_y(turn):
        return lax.rem(y + 1 + turn, NY)

    def columns_of(turn):
        return pl.ds(pl.multiple_of(turn_y(turn) * PART, PART), PART)

    def weight_gradient(ahead, turn):
        at = lax.rem(zl + ahead, SEG)
        first = pl.multiple_of(at * QUART + turn_y(turn) * PART, PART)
        total = dot(g_t[:, :ROWS], xbuf[0, :, pl.ds(first, PART)])
        total = total + dot(g_t[:, ROWS:], xtail[0, :, pl.ds(first, PART)])
        dw[at, :, columns_of(turn)] = total

    def own_term(dest, kind, turn):
        row = pl.multiple_of(kind * WIDTH + (dest // SEG) * SUB, SUB)
        return dw[lax.rem(dest, SEG), pl.ds(row, SUB), columns_of(turn)]

    def sum_part(ref, step, way, turn):
        if step == 0:
            return ref.at[way, step, turn, way * SUB : (way + 1) * SUB, :]
        return ref.at[way, step, turn]

    def sum_in(step, way, turn):
        ref = sum_part(rs_in, step, way, turn)
        arrived(ref, r_s.at[way, step, turn], r_r.at[way, step, turn])

    def came(step, way, turn, kind):
        return rs_in[way, step, turn, kind * SUB : (kind + 1) * SUB, :].astype(F32)

    def sum_on(step, turn):
        for way in range(2):
            if step > 1:
                sum_in(step - 1, way, turn)
            if step == 2:
                sum_in(0, way, turn)
            ahead = STEPS - step if way == 0 else NZ - STEPS + step
            for kind in range(2):
                if step == 0 and kind != way:
                    continue
                total = own_term(lax.rem(z + ahead, NZ), kind, turn)
                if step > 1:
                    total = total + came(step - 1, way, turn, kind)
                if step == 2 and kind == way:
                    total = total + came(0, way, turn, kind)
                rows = slice(kind * SUB, (kind + 1) * SUB)
                rs_out[way, step, turn, rows, :] = total.astype(BF16)
            send(
                sum_part(rs_out, step, way, turn),
                sum_part(rs_in, step, way, turn),
                r_s.at[way, step, turn],
                r_r.at[way, step, turn],
                (over_z if step == 0 else to_z)[way],
            )

    own_sum = pltpu.make_async_copy(fin_out.at[p], fin_in.at[p], load_sem.at[3])

    def sum_out(turn):
        for way in range(2):
            sum_in(STEPS - 1, way, turn)
        to_y_here = turn_y(turn)
        for kind in range(2):
            total = own_term(z, kind, turn)
            for way in range(2):
                total = total + came(STEPS - 1, way, turn, kind)
            total = total.astype(BF16)
            for core in range(NC):
                fin_out[to_y_here * NC + core, kind * SUB : (kind + 1) * SUB, :] = total[
                    :, core * FEAT : (core + 1) * FEAT
                ]
        for other in range(NC):
            if turn == NY - 1 and other == 0:
                own_sum.start()
                continue
            to = to_y_here * NC + lax.rem(c + other, NC)
            sems = f_s.at[turn, other], f_r.at[turn, other]
            send(fin_out.at[to], fin_in.at[p], *sems, member(to))

    for turn in range(NY):
        weight_gradient(0, turn)
        sum_on(0, turn)
        weight_gradient(1, turn)
        weight_gradient(3, turn)
        sum_on(1, turn)
    for turn in range(NY):
        weight_gradient(2, turn)
        sum_on(2, turn)
    for step in range(3, STEPS):
        for turn in range(NY):
            sum_on(step, turn)
    for turn in range(NY):
        sum_out(turn)
    for one in started:
        one.wait_send()
    own_sum.wait()
    for turn in range(NY):
        for other in range(NC):
            if turn == NY - 1 and other == 0:
                continue
            origin = lax.rem(y + NY - 1 - turn, NY) * NC + lax.rem(c + other, NC)
            arrived(fin_in.at[origin], f_s.at[turn, other], f_r.at[turn, other])


def finish(sums_ref, codes_ref, grad_ref, scale_ref):
    to_block = (iota((8, FEAT), 1) // BLOCK == iota((8, FEAT), 0)).astype(F32)
    for kind in range(2):
        summed = jnp.concatenate(
            [sums_ref[m, kind * SUB : (kind + 1) * SUB, :] for m in range(POOL)], axis=0
        ).astype(F32)
        codes = codes_ref[kind * HID : (kind + 1) * HID, :]
        grad_ref[kind * HID : (kind + 1) * HID, :] = jnp.where(codes % 8 != 7, summed, 0.0)
        blocks = lax.dot_general(
            to_block,
            summed * decode_values(codes),
            (((1,), (1,)), ((), ())),
            precision=lax.Precision.HIGHEST,
            preferred_element_type=F32,
        )
        scale_ref[kind] = LSQ * blocks[: FEAT // BLOCK]

def body(tokens, cotangent, routes, combine, gu_codes, gu_scales, d_codes, d_scales):
    hidden, width = gu_codes.shape[1], gu_codes.shape[2]
    vmem = pl.BlockSpec(memory_space=pltpu.VMEM)
    hbm = pl.BlockSpec(memory_space=pl.ANY)
    dma = pltpu.SemaphoreType.DMA
    codes = gu_codes.reshape(2 * hidden, width)
    sums = pl.pallas_call(
        kernel,
        out_shape=jax.ShapeDtypeStruct((POOL, 2 * SUB, FEAT), BF16),
        in_specs=[hbm] * 8,
        out_specs=hbm,
        scratch_shapes=[
            pltpu.VMEM((TOK, D), BF16),
            pltpu.VMEM((TOK, D), BF16),
            pltpu.VMEM(routes.shape[::-1], jnp.int32),
            pltpu.VMEM(combine.shape[::-1], F32),
            pltpu.VMEM((2 * hidden, width), jnp.int32),
            pltpu.VMEM((2, width // BLOCK, hidden), F32),
            pltpu.VMEM(d_codes.shape, jnp.int32),
            pltpu.VMEM(d_scales.shape, F32),
            pltpu.VMEM((2, NX * MAIN, PACK), BF16),
            pltpu.VMEM((2, ROWS, PACK), BF16),
            pltpu.VMEM((2, TAILS, D), BF16),
            pltpu.VMEM((POOL, PIECE, FEAT), BF16),
            pltpu.VMEM((SEG * PIECE, D), BF16),
            pltpu.VMEM((NX, PMAIN + PTAIL, 3 * WIDTH), F32),
            pltpu.VMEM((TAILS, 3 * WIDTH), F32),
            pltpu.VMEM((2 * WIDTH, ROWS + TAILS), BF16),
            pltpu.VMEM((SEG, 2 * WIDTH, QUART), F32),
            pltpu.VMEM((2, STEPS, NY, 2 * SUB, PART), BF16),
            pltpu.VMEM((2, STEPS, NY, 2 * SUB, PART), BF16),
            pltpu.VMEM((POOL, 2 * SUB, FEAT), BF16),
            dma((12,)),
            dma((2, NX - 1)),
            dma((2, NX - 1)),
            dma((3, 2, NX)),
            dma((3, 2, NX)),
            dma((NX, 6)),
            dma((NX, 6)),
            dma((POOL - 1,)),
            dma((POOL - 1,)),
            dma((2, STEPS, 2)),
            dma((2, STEPS, 2)),
            dma((2, STEPS, NY)),
            dma((2, STEPS, NY)),
            dma((NY, NC)),
            dma((NY, NC)),
        ],
        compiler_params=pltpu.CompilerParams(
            collective_id=0, has_side_effects=True, vmem_limit_bytes=56 << 20
        ),
        cost_estimate=pl.CostEstimate(
            flops=2 * 640 * D * 5 * WIDTH, bytes_accessed=8 << 20, transcendentals=0
        ),
    )(
        tokens,
        cotangent,
        routes.T,
        combine.T,
        codes,
        gu_scales.swapaxes(1, 2),
        d_codes,
        d_scales,
    )
    grad, scale = pl.pallas_call(
        finish,
        out_shape=(
            jax.ShapeDtypeStruct((2 * hidden, width), F32),
            jax.ShapeDtypeStruct((2, width // BLOCK, hidden), F32),
        ),
        in_specs=[vmem] * 2,
        out_specs=(vmem, vmem),
    )(sums, codes)
    return (
        grad.reshape(2, hidden, width),
        scale.swapaxes(1, 2),
    )


def solution(mesh):
    rows = P(("dp", "tensor"), None)
    return jax.shard_map(
        body,
        mesh=mesh,
        in_specs=(
            rows,
            rows,
            rows,
            rows,
            P(None, "tensor", "dp"),
            P(None, "tensor", "dp"),
            P("tensor", "dp"),
            P("tensor", "dp"),
        ),
        out_specs=(P(None, "tensor", "dp"), P(None, "tensor", "dp")),
        check_vma=False,
    )
```

```python
import jax
import jax.numpy as jnp
from jax import lax
from jax.experimental import pallas as pl
from jax.experimental.pallas import tpu as pltpu
from jax.sharding import PartitionSpec as P

BLOCK = 32
CAP = 20
NX, NY, NZ, NC = 4, 4, 16, 2
SEG = 4
POOL = NY * NC
D = 4096
TOK = 256
MAIN = 16
TAIL = CAP - MAIN
QUART = D // SEG
PACK = D + QUART
HID = 256
SUB = HID // POOL
FEAT = 128
PIECE = 3 * SUB
HALF = PIECE // 2
PMAIN = POOL * MAIN
PTAIL = POOL * TAIL
ROWS = NX * PMAIN
TAILS = NX * PTAIL
WIDTH = SEG * SUB
OFFSETS = (0, 1, 3, 2)
STEPS = NZ // 2
PART = QUART // NY
MESH = pl.DeviceIdType.MESH
LSQ = 192.0 ** (-0.5)
F32 = jnp.float32
BF16 = jnp.bfloat16


def decode_values(code_array):
    modulus = (code_array % 8).astype(F32)
    levels = jnp.where(
        modulus < 4.0,
        0.5 * modulus,
        jnp.where(modulus < 6.0, modulus - 2.0, jnp.where(modulus < 7.0, 4.0, 6.0)),
    )
    return jnp.where(code_array >= 8, -levels, levels)


def iota(shape, axis):
    return lax.broadcasted_iota(jnp.int32, shape, axis)


def nt_dot(a, b):
    return lax.dot_general(a, b, (((1,), (1,)), ((), ())), preferred_element_type=F32)


def dot(a, b):
    return jnp.dot(a, b, preferred_element_type=F32)


def device_at(x, y, z, c):
    return (y * (SEG * NC) + lax.rem(z, SEG) * NC + c, x * SEG + z // SEG)


def kernel(
    tok_hbm,
    cot_hbm,
    routes_hbm,
    combine_hbm,
    gu_codes_hbm,
    gu_scales_hbm,
    d_codes_hbm,
    d_scales_hbm,
    fin_in,
    tok_v,
    cot_v,
    routes_ref,
    combine_ref,
    gu_codes_ref,
    gu_scales_ref,
    d_codes_ref,
    d_scales_ref,
    sbuf,
    xbuf,
    xtail,
    wsend,
    wfull,
    pre,
    pre_tail,
    g_t,
    dw,
    rs_out,
    rs_in,
    fin_out,
    load_sem,
    x_s,
    x_r,
    y_s,
    y_r,
    p_s,
    p_r,
    a_s,
    a_r,
    w_s,
    w_r,
    r_s,
    r_r,
    f_s,
    f_r,
):
    dp = lax.axis_index("dp")
    tensor = lax.axis_index("tensor")
    x, zh = tensor // SEG, lax.rem(tensor, SEG)
    y, rest = dp // (SEG * NC), lax.rem(dp, SEG * NC)
    zl, c = rest // NC, lax.rem(rest, NC)
    z = zh * SEG + zl
    p = y * NC + c
    oc = 1 - c
    y_up, y_dn, y_far = lax.rem(y + 1, NY), lax.rem(y + NY - 1, NY), lax.rem(y + 2, NY)
    z_up, z_dn = lax.rem(z + 1, NZ), lax.rem(z + NZ - 1, NZ)
    to_y = (device_at(x, y_up, z, c), device_at(x, y_dn, z, c))
    to_z = (device_at(x, y, z_up, c), device_at(x, y, z_dn, c))
    over_z = (
        device_at(x, y, lax.rem(z + 2, NZ), c),
        device_at(x, y, lax.rem(z + NZ - 2, NZ), c),
    )
    partner = device_at(x, y, z, oc)

    def member(index):
        return device_at(x, index // NC, z, lax.rem(index, NC))

    def copy(src, dst, sent, got, device):
        return pltpu.make_async_remote_copy(
            src_ref=src,
            dst_ref=dst,
            send_sem=sent,
            recv_sem=got,
            device_id=device,
            device_id_type=MESH,
        )

    started = []

    def send(src, dst, sent, got, device):
        one = copy(src, dst, sent, got, device)
        one.start()
        started.append(one)

    def arrived(dst, sent, got):
        copy(dst, dst, sent, got, partner).wait_recv()

    barrier = pltpu.get_barrier_semaphore()
    peers = [member(lax.rem(p + k, POOL)) for k in range(1, POOL)]
    peers += [device_at(lax.rem(x + o, NX), y, z, c) for o in range(1, NX)]
    peers += list(to_z) + list(over_z)
    for peer in peers:
        pl.semaphore_signal(barrier, inc=1, device_id=peer, device_id_type=MESH)

    pairs = (
        (gu_codes_hbm, gu_codes_ref),
        (gu_scales_hbm, gu_scales_ref),
        (d_codes_hbm, d_codes_ref),
        (d_scales_hbm, d_scales_ref),
        (routes_hbm, routes_ref),
        (combine_hbm, combine_ref),
        (tok_hbm, tok_v),
        (cot_hbm, cot_v),
    )
    loads = [
        pltpu.make_async_copy(src, dst, load_sem.at[4 + i])
        for i, (src, dst) in enumerate(pairs)
    ]
    for one in loads:
        one.start()

    def piece(origin, first=0, count=PIECE):
        row = pl.multiple_of((origin // SEG) * PIECE + first, 16)
        column = pl.multiple_of(lax.rem(origin, SEG) * QUART, QUART)
        return wfull.at[pl.ds(row, count), pl.ds(column, QUART)]

    def part(index):
        row = pl.multiple_of(zh * PIECE, 16)
        column = pl.multiple_of(zl * QUART + index * FEAT, FEAT)
        return wfull.at[pl.ds(row, PIECE), pl.ds(column, FEAT)]

    def for_expert(which, e):
        return sbuf.at[which, pl.ds(pl.multiple_of(e * MAIN, MAIN), MAIN), :]

    def rows_of(group, at_y, at_c):
        row = group * PMAIN + (at_y * NC + at_c) * MAIN
        return pl.ds(pl.multiple_of(row, MAIN), MAIN)

    def block(group, at_y, at_c):
        return xbuf.at[:, rows_of(group, at_y, at_c), :]

    def one_block(which, group, at_y, at_c):
        return xbuf.at[which, rows_of(group, at_y, at_c), :]

    def own_part_of(which, group):
        return one_block(which, group, y, c)

    def spread(which, group):
        if group == 0:
            source = for_expert(which, x)
        else:
            source = own_part_of(which, group)
            arrived(source, x_s.at[which, group - 1], x_r.at[which, group - 1])
        for way in range(2):
            send(
                source,
                own_part_of(which, group),
                y_s.at[which, way, group],
                y_r.at[which, way, group],
                to_y[way],
            )
        sems = p_s.at[group, 5 * which], p_r.at[group, 5 * which]
        send(source, own_part_of(which, group), *sems, partner)

    for one in loads[:4]:
        one.wait()
    lane_block = iota((HID, FEAT), 1) // BLOCK
    for g in range(2):
        rows = pl.ds(g * HID, HID)
        padding = jnp.zeros((FEAT - FEAT // BLOCK, HID), F32)
        turned = jnp.concatenate([gu_scales_ref[g], padding], axis=0).T
        scale = jnp.zeros((HID, FEAT), F32)
        for b in range(FEAT // BLOCK):
            scale = jnp.where(lane_block == b, turned[:, b : b + 1], scale)
        weight = (scale * decode_values(gu_codes_ref[rows, :])).astype(BF16)
        for m in range(POOL):
            wsend[m, g * SUB : (g + 1) * SUB, :] = weight[m * SUB : (m + 1) * SUB, :]
    for m in range(POOL):
        values = decode_values(d_codes_ref[m * SUB : (m + 1) * SUB, :])
        wsend[m, 2 * SUB : 3 * SUB, :] = (d_scales_ref[m : m + 1, :] * values).astype(BF16)

    pl.semaphore_wait(barrier, len(peers))
    own_part = pltpu.make_async_copy(wsend.at[p], part(p), load_sem.at[2])
    own_part.start()
    for k in range(1, POOL):
        to = lax.rem(p + k, POOL)
        send(wsend.at[to], part(p), a_s.at[k - 1], a_r.at[k - 1], member(to))

    loads[4].wait()
    loads[5].wait()
    masks, weights = [], []
    for e in range(NX):
        chosen = routes_ref[...] == e
        masks.append(jnp.max(chosen.astype(F32), axis=0, keepdims=True))
        weights.append(
            jnp.sum(jnp.where(chosen, combine_ref[...], 0.0), axis=0, keepdims=True)
        )
    mask = jnp.concatenate(masks + [jnp.zeros((4, TOK), F32)], axis=0)
    before = (iota((TOK, TOK), 0) <= iota((TOK, TOK), 1)).astype(F32).astype(BF16)
    count = dot(mask.astype(BF16), before)
    place = jnp.where(mask > 0.0, count - 1.0, -1.0).astype(jnp.int32)
    wide = (MAIN, TOK)
    place = jnp.concatenate(
        [jnp.broadcast_to(place[e : e + 1], wide) for e in range(NX)], axis=0
    )
    weight = jnp.concatenate(
        [jnp.broadcast_to(weights[e], wide) for e in range(NX)], axis=0
    )
    slot = lax.rem(iota((NX * MAIN, TOK), 0), MAIN)
    is_main = place == slot
    is_tail = place == MAIN + lax.rem(slot, TAIL)
    main_weight = jnp.sum(jnp.where(is_main, weight, 0.0), axis=1, keepdims=True)
    tail_weight = jnp.sum(jnp.where(is_tail, weight, 0.0), axis=1, keepdims=True)
    pick_main = is_main.astype(F32).astype(BF16)
    picks = []
    for k in range(SEG):
        pick_tail = (is_tail & (slot // TAIL == k)).astype(F32).astype(BF16)
        picks.append(jnp.concatenate([pick_main, pick_tail], axis=0))

    wide = QUART // NY
    own_rows = []
    for which, (source, load) in enumerate(((tok_v, loads[6]), (cot_v, loads[7]))):
        load.wait()
        for quarter in range(NY):
            folded = jnp.zeros((NX * MAIN, wide), F32)
            for k in range(SEG):
                first = quarter * QUART + k * wide
                both = dot(picks[k], source[:, first : first + wide])
                picked = both[: NX * MAIN]
                folded = folded + both[NX * MAIN :]
                if which == 1:
                    picked = picked * main_weight
                to = k * QUART + quarter * wide
                sbuf[which, :, to : to + wide] = picked.astype(BF16)
            if which == 1:
                folded = folded * tail_weight
            to = D + quarter * wide
            sbuf[which, :, to : to + wide] = folded.astype(BF16)
        for group in range(1, NX):
            e = lax.rem(x + OFFSETS[group], NX)
            send(
                for_expert(which, e),
                own_part_of(which, group),
                x_s.at[which, group - 1],
                x_r.at[which, group - 1],
                device_at(e, y, z, c),
            )
        spread(which, 0)
        own_rows.append(
            pltpu.make_async_copy(
                for_expert(which, x), own_part_of(which, 0), load_sem.at[which]
            )
        )
        own_rows[which].start()

    def relay(group):
        for way in range(2):
            from_y = (y_dn, y_up)[way]
            whole = block(group, from_y, c)
            for which in (way, 1 - way):
                half = one_block(which, group, from_y, c)
                arrived(half, y_s.at[which, way, group], y_r.at[which, way, group])
                if which == way:
                    sems = y_s.at[2, way, group], y_r.at[2, way, group]
                    send(half, half, *sems, to_y[way])
            send(whole, whole, p_s.at[group, 1 + way], p_r.at[group, 1 + way], partner)

    def relay_far(group):
        for way in range(2):
            half = one_block(way, group, y_far, c)
            arrived(half, y_s.at[2, way, group], y_r.at[2, way, group])
            send(half, half, p_s.at[group, 3 + way], p_r.at[group, 3 + way], partner)

    def all_rows(group):
        for which in range(2):
            half = one_block(which, group, y, oc)
            arrived(half, p_s.at[group, 5 * which], p_r.at[group, 5 * which])
        arrived(block(group, y_dn, oc), p_s.at[group, 1], p_r.at[group, 1])
        arrived(block(group, y_up, oc), p_s.at[group, 2], p_r.at[group, 2])
        for way in range(2):
            half = one_block(way, group, y_far, oc)
            arrived(half, p_s.at[group, 3 + way], p_r.at[group, 3 + way])

    def ways_of(step, half):
        return range(2) if step < STEPS else (half,)

    def weights_on(step, half):
        for way in ways_of(step, half):
            back = NZ - (step - 1) if way == 0 else step - 1
            ref = piece(lax.rem(z + back, NZ), half * HALF, HALF)
            sems = w_s.at[way, step - 1, half], w_r.at[way, step - 1, half]
            send(ref, ref, *sems, to_z[way])

    def weights_in(step, half):
        for way in ways_of(step, half):
            back = NZ - step if way == 0 else step
            ref = piece(lax.rem(z + back, NZ), half * HALF, HALF)
            arrived(ref, w_s.at[way, step - 1, half], w_r.at[way, step - 1, half])
        if step < STEPS:
            weights_on(step + 1, half)

    fold_from = iota((PMAIN, PMAIN), 1)
    fold_to = iota((PMAIN, PMAIN), 0)
    inside = lax.rem(fold_to, PTAIL)
    wanted = (inside // TAIL) * MAIN + (fold_to // PTAIL) * TAIL + lax.rem(inside, TAIL)
    unfold = (fold_from == wanted).astype(F32).astype(BF16)

    def unpack(group):
        all_rows(group)
        for which in range(2):
            folded = xbuf[which, group * PMAIN : (group + 1) * PMAIN, D:PACK]
            tails = dot(unfold, folded).astype(BF16)
            for k in range(SEG):
                xtail[
                    which,
                    group * PTAIL : (group + 1) * PTAIL,
                    k * QUART : (k + 1) * QUART,
                ] = tails[k * PTAIL : (k + 1) * PTAIL, :]

    def gradients(gate, up, back):
        sig = jax.nn.sigmoid(gate)
        to_gate = back * up * sig * (1.0 + gate * (1.0 - sig))
        to_up = back * (gate * sig)
        return to_gate.T.astype(BF16), to_up.T.astype(BF16)

    def forward(group, quarters, first, last):
        rows = pl.ds(group * PMAIN, PMAIN)
        tails = pl.ds(group * PTAIL, PTAIL)
        count = PMAIN + PTAIL
        if first:
            front = jnp.zeros((count, 2 * WIDTH), F32)
            back = jnp.zeros((count, WIDTH), F32)
        else:
            front, back = pre[group, :, : 2 * WIDTH], pre[group, :, 2 * WIDTH :]
        for quarter in quarters:
            at = pl.multiple_of(lax.rem(zl + quarter, SEG) * QUART, QUART)
            columns = pl.ds(at, QUART)

            def side(kind):
                return [
                    wfull[q * PIECE + kind * SUB : q * PIECE + (kind + 1) * SUB, columns]
                    for q in range(SEG)
                ]

            gate_up = jnp.concatenate(side(0) + side(1), axis=0)
            down = jnp.concatenate(side(2), axis=0)
            tokens = jnp.concatenate([xbuf[0, rows, columns], xtail[0, tails, columns]], 0)
            scaled = jnp.concatenate([xbuf[1, rows, columns], xtail[1, tails, columns]], 0)
            front = front + nt_dot(tokens, gate_up)
            back = back + nt_dot(scaled, down)
        if not last:
            pre[group, :, : 2 * WIDTH] = front
            pre[group, :, 2 * WIDTH :] = back
            return
        to_gate, to_up = gradients(
            front[:PMAIN, :WIDTH], front[:PMAIN, WIDTH:], back[:PMAIN]
        )
        g_t[:WIDTH, rows] = to_gate
        g_t[WIDTH:, rows] = to_up
        pre_tail[tails, : 2 * WIDTH] = front[PMAIN:]
        pre_tail[tails, 2 * WIDTH :] = back[PMAIN:]

    own_part.wait()
    for k in range(1, POOL):
        got = part(lax.rem(p + POOL - k, POOL))
        arrived(got, a_s.at[k - 1], a_r.at[k - 1])
    weights_on(1, 0)
    weights_on(1, 1)

    weights_in(1, 0)
    spread(0, 1)
    spread(0, 2)
    weights_in(1, 1)
    relay(0)
    spread(0, 3)
    weights_in(2, 0)
    weights_in(2, 1)
    spread(1, 1)
    spread(1, 2)
    weights_in(3, 0)
    weights_in(3, 1)
    spread(1, 3)
    weights_in(4, 0)
    weights_in(4, 1)
    for one in own_rows:
        one.wait()
    weights_in(5, 0)
    weights_in(5, 1)
    relay(1)
    weights_in(6, 0)
    relay_far(0)
    weights_in(6, 1)
    relay(2)
    unpack(0)
    forward(0, (2,), True, False)
    weights_in(7, 0)
    weights_in(7, 1)
    forward(0, (1, 3), False, False)
    relay(3)
    relay_far(1)
    unpack(1)
    forward(1, (2, 1, 3), True, False)
    relay_far(2)
    unpack(2)
    forward(2, (2, 1, 3), True, False)
    weights_in(8, 0)
    weights_in(8, 1)
    forward(0, (0,), False, True)
    forward(1, (0,), False, True)
    forward(2, (0,), False, True)
    relay_far(3)
    unpack(3)
    forward(3, (0, 1, 2, 3), True, True)
    to_gate, to_up = gradients(
        pre_tail[:, :WIDTH], pre_tail[:, WIDTH : 2 * WIDTH], pre_tail[:, 2 * WIDTH :]
    )
    g_t[:WIDTH, ROWS:] = to_gate
    g_t[WIDTH:, ROWS:] = to_up

    def turn_y(turn):
        return lax.rem(y + 1 + turn, NY)

    def columns_of(turn):
        return pl.ds(pl.multiple_of(turn_y(turn) * PART, PART), PART)

    def weight_gradient(ahead, turn):
        at = lax.rem(zl + ahead, SEG)
        first = pl.multiple_of(at * QUART + turn_y(turn) * PART, PART)
        total = dot(g_t[:, :ROWS], xbuf[0, :, pl.ds(first, PART)])
        total = total + dot(g_t[:, ROWS:], xtail[0, :, pl.ds(first, PART)])
        dw[at, :, columns_of(turn)] = total

    def own_term(dest, kind, turn):
        row = pl.multiple_of(kind * WIDTH + (dest // SEG) * SUB, SUB)
        return dw[lax.rem(dest, SEG), pl.ds(row, SUB), columns_of(turn)]

    def sum_part(ref, step, way, turn):
        if step == 0:
            return ref.at[way, step, turn, way * SUB : (way + 1) * SUB, :]
        return ref.at[way, step, turn]

    def sum_in(step, way, turn):
        ref = sum_part(rs_in, step, way, turn)
        arrived(ref, r_s.at[way, step, turn], r_r.at[way, step, turn])

    def came(step, way, turn, kind):
        return rs_in[way, step, turn, kind * SUB : (kind + 1) * SUB, :].astype(F32)

    def sum_on(step, turn):
        for way in range(2):
            if step > 1:
                sum_in(step - 1, way, turn)
            if step == 2:
                sum_in(0, way, turn)
            ahead = STEPS - step if way == 0 else NZ - STEPS + step
            for kind in range(2):
                if step == 0 and kind != way:
                    continue
                total = own_term(lax.rem(z + ahead, NZ), kind, turn)
                if step > 1:
                    total = total + came(step - 1, way, turn, kind)
                if step == 2 and kind == way:
                    total = total + came(0, way, turn, kind)
                rows = slice(kind * SUB, (kind + 1) * SUB)
                rs_out[way, step, turn, rows, :] = total.astype(BF16)
            send(
                sum_part(rs_out, step, way, turn),
                sum_part(rs_in, step, way, turn),
                r_s.at[way, step, turn],
                r_r.at[way, step, turn],
                (over_z if step == 0 else to_z)[way],
            )

    own_sum = pltpu.make_async_copy(fin_out.at[p], fin_in.at[p], load_sem.at[3])

    def sum_out(turn):
        for way in range(2):
            sum_in(STEPS - 1, way, turn)
        to_y_here = turn_y(turn)
        for kind in range(2):
            total = own_term(z, kind, turn)
            for way in range(2):
                total = total + came(STEPS - 1, way, turn, kind)
            total = total.astype(BF16)
            for core in range(NC):
                fin_out[to_y_here * NC + core, kind * SUB : (kind + 1) * SUB, :] = total[
                    :, core * FEAT : (core + 1) * FEAT
                ]
        for other in range(NC):
            if turn == NY - 1 and other == 0:
                own_sum.start()
                continue
            to = to_y_here * NC + lax.rem(c + other, NC)
            sems = f_s.at[turn, other], f_r.at[turn, other]
            send(fin_out.at[to], fin_in.at[p], *sems, member(to))

    for turn in range(NY):
        weight_gradient(0, turn)
        sum_on(0, turn)
        weight_gradient(1, turn)
        weight_gradient(3, turn)
        sum_on(1, turn)
    for turn in range(NY):
        weight_gradient(2, turn)
        sum_on(2, turn)
    for step in range(3, STEPS):
        for turn in range(NY):
            sum_on(step, turn)
    for turn in range(NY):
        sum_out(turn)
    for one in started:
        one.wait_send()
    own_sum.wait()
    for turn in range(NY):
        for other in range(NC):
            if turn == NY - 1 and other == 0:
                continue
            origin = lax.rem(y + NY - 1 - turn, NY) * NC + lax.rem(c + other, NC)
            arrived(fin_in.at[origin], f_s.at[turn, other], f_r.at[turn, other])


def finish(sums_ref, codes_ref, grad_ref, scale_ref):
    to_block = (iota((8, FEAT), 1) // BLOCK == iota((8, FEAT), 0)).astype(F32)
    for kind in range(2):
        summed = jnp.concatenate(
            [sums_ref[m, kind * SUB : (kind + 1) * SUB, :] for m in range(POOL)], axis=0
        ).astype(F32)
        codes = codes_ref[kind * HID : (kind + 1) * HID, :]
        grad_ref[kind * HID : (kind + 1) * HID, :] = jnp.where(codes % 8 != 7, summed, 0.0)
        blocks = lax.dot_general(
            to_block,
            summed * decode_values(codes),
            (((1,), (1,)), ((), ())),
            precision=lax.Precision.HIGHEST,
            preferred_element_type=F32,
        )
        scale_ref[kind] = LSQ * blocks[: FEAT // BLOCK]

def body(tokens, cotangent, routes, combine, gu_codes, gu_scales, d_codes, d_scales):
    hidden, width = gu_codes.shape[1], gu_codes.shape[2]
    vmem = pl.BlockSpec(memory_space=pltpu.VMEM)
    hbm = pl.BlockSpec(memory_space=pl.ANY)
    dma = pltpu.SemaphoreType.DMA
    codes = gu_codes.reshape(2 * hidden, width)
    sums = pl.pallas_call(
        kernel,
        out_shape=jax.ShapeDtypeStruct((POOL, 2 * SUB, FEAT), BF16),
        in_specs=[hbm] * 8,
        out_specs=hbm,
        scratch_shapes=[
            pltpu.VMEM((TOK, D), BF16),
            pltpu.VMEM((TOK, D), BF16),
            pltpu.VMEM(routes.shape[::-1], jnp.int32),
            pltpu.VMEM(combine.shape[::-1], F32),
            pltpu.VMEM((2 * hidden, width), jnp.int32),
            pltpu.VMEM((2, width // BLOCK, hidden), F32),
            pltpu.VMEM(d_codes.shape, jnp.int32),
            pltpu.VMEM(d_scales.shape, F32),
            pltpu.VMEM((2, NX * MAIN, PACK), BF16),
            pltpu.VMEM((2, ROWS, PACK), BF16),
            pltpu.VMEM((2, TAILS, D), BF16),
            pltpu.VMEM((POOL, PIECE, FEAT), BF16),
            pltpu.VMEM((SEG * PIECE, D), BF16),
            pltpu.VMEM((NX, PMAIN + PTAIL, 3 * WIDTH), F32),
            pltpu.VMEM((TAILS, 3 * WIDTH), F32),
            pltpu.VMEM((2 * WIDTH, ROWS + TAILS), BF16),
            pltpu.VMEM((SEG, 2 * WIDTH, QUART), F32),
            pltpu.VMEM((2, STEPS, NY, 2 * SUB, PART), BF16),
            pltpu.VMEM((2, STEPS, NY, 2 * SUB, PART), BF16),
            pltpu.VMEM((POOL, 2 * SUB, FEAT), BF16),
            dma((12,)),
            dma((2, NX - 1)),
            dma((2, NX - 1)),
            dma((3, 2, NX)),
            dma((3, 2, NX)),
            dma((NX, 6)),
            dma((NX, 6)),
            dma((POOL - 1,)),
            dma((POOL - 1,)),
            dma((2, STEPS, 2)),
            dma((2, STEPS, 2)),
            dma((2, STEPS, NY)),
            dma((2, STEPS, NY)),
            dma((NY, NC)),
            dma((NY, NC)),
        ],
        compiler_params=pltpu.CompilerParams(
            collective_id=0, has_side_effects=True, vmem_limit_bytes=56 << 20
        ),
        cost_estimate=pl.CostEstimate(
            flops=2 * 640 * D * 5 * WIDTH, bytes_accessed=8 << 20, transcendentals=0
        ),
    )(
        tokens,
        cotangent,
        routes.T,
        combine.T,
        codes,
        gu_scales.swapaxes(1, 2),
        d_codes,
        d_scales,
    )
    grad, scale = pl.pallas_call(
        finish,
        out_shape=(
            jax.ShapeDtypeStruct((2 * hidden, width), F32),
            jax.ShapeDtypeStruct((2, width // BLOCK, hidden), F32),
        ),
        in_specs=[vmem] * 2,
        out_specs=(vmem, vmem),
    )(sums, codes)
    return (
        grad.reshape(2, hidden, width),
        scale.swapaxes(1, 2),
    )


def solution(mesh):
    rows = P(("dp", "tensor"), None)
    return jax.shard_map(
        body,
        mesh=mesh,
        in_specs=(
            rows,
            rows,
            rows,
            rows,
            P(None, "tensor", "dp"),
            P(None, "tensor", "dp"),
            P("tensor", "dp"),
            P("tensor", "dp"),
        ),
        out_specs=(P(None, "tensor", "dp"), P(None, "tensor", "dp")),
        check_vma=False,
    )
```
